512 devices in a mesh: dp: 128 (over y, z, core), helper: 4 (over x).
Axes of the slice: x: 4, y: 4, z: 16, core: 2. Of those that a mesh axis runs over, the one named last changes fastest.
Arguments:
- embeddings: bfloat16 [131072, 768], P(('dp', 'helper')), may hold values from -70 to 70
- cluster: int32 [131072], P(('dp', 'helper')), may hold values from 0 to 127, as said below
- order_rank: int32 [131072], P(('dp', 'helper')), may hold values from 0 to 1023
Outputs:
- nearest_earlier: float32 [131072], P(('dp', 'helper'))
The draws below stay inside these ranges and needn't reach their ends.
Inputs may be any that keep to these rules, and one draw needn't show every extreme that they name: Among the rows of one device at most 4 name the same cluster; in every draw one cluster is named by exactly 4 rows of every device.
All inputs are finite; a program needn't handle non-finite values.
Results may differ from the reference program's by a relative error of at most 0.00053.
Values may be sent and summed in bfloat16 or wider, within the bound.
A program may use at most 64 MiB of HBM per device.

```python
import math
import jax
import jax.numpy as jnp
from jax import lax

D = 768
R_DEV = 256
CLUSTERS = 128
ROWS = 131072
SLOT_C = 4
N_DP = 128
N_HELPER = 4


def cluster_plan(key):
    base = jax.random.fold_in(key, 101)
    token_total = CLUSTERS * SLOT_C
    token_holder = jnp.arange(token_total, dtype=jnp.int32) // SLOT_C
    weights = jnp.left_shift(jnp.int32(1), jax.random.randint(jax.random.fold_in(base, 1), (CLUSTERS,), 0, 4))
    dominant_rows = jax.random.randint(jax.random.fold_in(base, 2), (), 0, CLUSTERS)

    def one_block(block_key):
        local_dominant = jax.random.randint(jax.random.fold_in(block_key, 1), (), 0, CLUSTERS)
        unadjusted_score = jax.random.randint(jax.random.fold_in(block_key, 2), (token_total,), 0, 4096) * weights[token_holder]
        extra_credit = jnp.where(token_holder == dominant_rows, 65536, 0) + jnp.where(token_holder == local_dominant, 32768, 0)
        score_values = (unadjusted_score + extra_credit) * 2048 + jnp.arange(token_total, dtype=jnp.int32)
        chosen = lax.top_k(score_values, R_DEV)[1]
        shuffled = jax.random.permutation(jax.random.fold_in(block_key, 3), chosen)
        return token_holder[shuffled]
    block_keys = jax.random.split(jax.random.fold_in(base, 3), ROWS // R_DEV)
    return jax.vmap(one_block)(block_keys).reshape(ROWS).astype(jnp.int32)


def draw_cluster(key, part):
    return cluster_plan(key)


def draw_embeddings(key, part):
    assigned = cluster_plan(key)
    key = jax.random.fold_in(key, 5)
    pair_count = ROWS // (2 * CLUSTERS)
    pair_ids = assigned * pair_count + jax.random.randint(jax.random.fold_in(key, 1), (ROWS,), 0, pair_count)
    pair_key = jax.random.fold_in(key, 2)
    centers = jnp.clip(jax.random.normal(jax.random.fold_in(key, 3), (CLUSTERS, D)), -4.0, 4.0)
    own_part = jnp.clip(jax.random.normal(jax.random.fold_in(key, 4), (ROWS, D)), -4.0, 4.0)
    shared = jax.vmap(lambda pair_id: jnp.clip(jax.random.normal(jax.random.fold_in(pair_key, pair_id), (D,)), -4.0, 4.0))(pair_ids)
    scales = jnp.exp(jax.random.uniform(jax.random.fold_in(key, 5), (ROWS, 1), minval=0.0, maxval=math.log(10.0)))
    mixed = scales * (0.6 * centers[assigned] + 0.5 * shared + 0.6 * own_part)
    return mixed.astype(jnp.bfloat16)


def set_ends(array, own_key, smallest, largest):
    index_at = [jax.random.randint(jax.random.fold_in(own_key, axis), (), 0, length) for axis, length in enumerate(array.shape)]
    longest = array.shape.index(max(array.shape))
    next_to = index_at[:longest] + [(index_at[longest] + 1) % array.shape[longest]] + index_at[longest + 1:]
    return array.at[tuple(index_at)].set(smallest).at[tuple(next_to)].set(largest)


def setup_inputs(seed: int = 0) -> dict:
    keys = jax.random.split(jax.random.key(seed), 4)
    return {
        "embeddings": draw_embeddings(jax.random.fold_in(keys[3], 71), 0),
        "cluster": draw_cluster(jax.random.fold_in(keys[3], 71), 0),
        "order_rank": set_ends(jax.random.randint(keys[2], (ROWS,), 0, 1024), jax.random.fold_in(keys[2], 1), 0, 1023).astype(jnp.int32),
    }


sentinel = 2147483647

def unit_rows(raw_rows):
    values = raw_rows.astype(jnp.float32)
    return (values * lax.rsqrt(lax.optimization_barrier(jnp.sum(values * values, axis=-1, keepdims=True)) + 1e-06)).astype(jnp.bfloat16)

def reference(embeddings, cluster, order_rank):
    unit_vecs = unit_rows(embeddings)
    row_ids = jnp.arange(ROWS, dtype=jnp.int32)
    order_key = order_rank * ROWS + row_ids
    arranged = jnp.argsort(cluster, stable=True).astype(jnp.int32)
    counts = jax.ops.segment_sum(jnp.ones((ROWS,), jnp.int32), cluster, num_segments=CLUSTERS)
    starts = jnp.cumsum(counts) - counts
    capacity = N_DP * N_HELPER * SLOT_C

    def one_cluster(cluster_at):
        positions = starts[cluster_at] + jnp.arange(capacity, dtype=jnp.int32)
        occupied = jnp.arange(capacity, dtype=jnp.int32) < counts[cluster_at]
        picked = arranged[jnp.minimum(positions, ROWS - 1)]
        rows_here = unit_vecs[picked]
        keys_here = jnp.where(occupied, order_key[picked], sentinel)
        score_values = jnp.dot(rows_here, rows_here.T, preferred_element_type=jnp.float32)
        earlier = keys_here[None, :] < keys_here[:, None]
        nearest = lax.optimization_barrier(jnp.max(jnp.where(earlier, score_values, jnp.float32(-1.0)), axis=1))
        return (jnp.where(occupied, picked, ROWS).astype(jnp.int32), nearest)
    targets, values = lax.map(one_cluster, jnp.arange(CLUSTERS, dtype=jnp.int32))
    result = jnp.full((ROWS,), -1.0, jnp.float32)
    return result.at[targets.reshape(-1)].set(values.reshape(-1), mode='drop')
```

```python
import functools

import jax
import jax.numpy as jnp
from jax import lax
from jax.experimental import pallas as pl
from jax.experimental.pallas import tpu as pltpu
from jax.sharding import PartitionSpec as P

MESH = pl.DeviceIdType.MESH
Y, Z, CORES, X = 4, 16, 2, 4
SLOTS = 4
BLOCK = CORES * SLOTS
ROWS_Z = Y * BLOCK
PANEL = Z * ROWS_Z
GROUP = 2
GROUPS = Z // GROUP
EMPTY = 8388608.0


def z_offset(index):
    return (index + 1) // 2 if index % 2 else -(index // 2)


def wait_bytes(ref, sem):
    pltpu.make_async_copy(ref, ref, sem).wait()


def iota(shape, dim):
    return lax.broadcasted_iota(jnp.int32, shape, dim)


def dot_t(lhs, rhs):
    return lax.dot_general(lhs, rhs, (((1,), (1,)), ((), ())), preferred_element_type=jnp.float32)


def kernel(
    emb_ref,
    cluster_ref,
    rank_ref,
    out_ref,
    units,
    meta,
    send_z,
    from_z,
    panels,
    key_send,
    key_z,
    key_y,
    key_x,
    key_cols,
    result,
    ret_z,
    ret_y,
    core_send,
    core_recv,
    z_send,
    z_recv,
    y_send,
    y_recv,
    x_send,
    x1_recv,
    x2_recv,
    x3_recv,
    key_send_sem,
    key_recv_sem,
    ret_send_sem,
    ret_recv_sem,
):
    dp, hx = lax.axis_index("dp"), lax.axis_index("helper")
    core, chip = dp % CORES, dp // CORES
    y, z = chip // Z, chip % Z

    def at(dy=0, dz=0, dx=0, dcore=0):
        chip_to = ((y + dy + Y) % Y) * Z + (z + dz + Z) % Z
        return (chip_to * CORES + (core + dcore) % CORES, (hx + dx + X) % X)

    def remote(src, dst, send_sem, recv_sem, to):
        pltpu.make_async_remote_copy(
            src_ref=src,
            dst_ref=dst,
            send_sem=send_sem,
            recv_sem=recv_sem,
            device_id=to,
            device_id_type=MESH,
        ).start()

    barrier = pltpu.get_barrier_semaphore()
    peers = [at(dz=z_offset(a)) for a in range(Z - 1, 0, -1)]
    peers += [at(dy=d) for d in range(1, Y)] + [at(dy=d, dcore=1) for d in range(Y)]
    peers += [at(dx=d) for d in range(1, X)]
    for peer in peers:
        pl.semaphore_signal(barrier, inc=1, device_id=peer, device_id_type=MESH)

    rows = emb_ref.shape[0]
    values = emb_ref[...].astype(jnp.float32)
    scale = lax.rsqrt(jnp.sum(values * values, axis=-1, keepdims=True) + 1e-06)
    units[core] = (values * scale).astype(jnp.bfloat16)

    cluster = cluster_ref[...].reshape(1, rows)
    rank = rank_ref[...].reshape(1, rows)
    across = jnp.broadcast_to(cluster, (rows, rows))
    down = jnp.transpose(across)
    same_before = (down == across) & (iota((rows, rows), 0) < iota((rows, rows), 1))
    slot = jnp.sum(same_before.astype(jnp.float32), axis=0, keepdims=True).astype(jnp.int32)
    owner_chip = cluster // CORES
    dy = (owner_chip // Z - y + Y) % Y
    dz = (owner_chip % Z - z + Z) % Z
    a_of = jnp.where(dz == 0, 0, jnp.where(dz <= Z // 2, 2 * dz - 1, 2 * (Z - dz)))
    target = a_of * ROWS_Z + dy * BLOCK + core * SLOTS + slot
    owner_core = cluster % CORES
    key = rank * (Z * Y * CORES * X * SLOTS) + (dp * X + hx) * SLOTS + slot + 1
    meta[core, 0:1, :] = (target + owner_core * PANEL).astype(jnp.float32)
    meta[core, 1:2, :] = (key // 16384).astype(jnp.float32)
    meta[core, 2:3, :] = (key // 128 % 128).astype(jnp.float32)
    meta[core, 3:4, :] = (key % 128).astype(jnp.float32)
    meta[core, 4:8, :] = jnp.zeros((4, rows), jnp.float32)

    pl.semaphore_wait(barrier, len(peers))
    remote(units.at[core], units.at[core], core_send.at[0], core_recv.at[0], at(dcore=1))
    remote(meta.at[core], meta.at[core], core_send.at[1], core_recv.at[1], at(dcore=1))
    wait_bytes(meta.at[0], core_recv.at[1])
    wait_bytes(units.at[0], core_recv.at[0])

    targets = [meta[c, 0:1, :].astype(jnp.int32) - core * PANEL for c in range(CORES)]
    chunk = 4 * ROWS_Z
    for first in range(Z - 4, -1, -4):
        picked = jnp.zeros((chunk, units.shape[2]), jnp.float32)
        for c in range(CORES):
            pick = (iota((chunk, rows), 0) + first * ROWS_Z == targets[c]).astype(jnp.float32)
            picked += jnp.dot(
                pick.astype(jnp.bfloat16), units[c], preferred_element_type=jnp.float32
            )
        picked = picked.astype(jnp.bfloat16).reshape(4, Y, BLOCK, units.shape[2])
        for i in range(3, -1, -1):
            a = first + i
            if a == 0:
                from_z[0] = picked[0]
            else:
                send_z[a] = picked[i]
                remote(
                    send_z.at[a],
                    from_z.at[a],
                    z_send,
                    z_recv.at[a // GROUP],
                    at(dz=z_offset(a)),
                )

    keys = jnp.zeros((Z, 128), jnp.float32)
    lane = iota((128, rows), 0)
    for c in range(CORES):
        here = (targets[c] >= 0) & (targets[c] < PANEL)
        row_a = jnp.where(here, targets[c] // ROWS_Z, -1)
        pick = (iota((Z, rows), 0) == row_a).astype(jnp.float32).astype(jnp.bfloat16)
        part = jnp.where(
            lane < ROWS_Z,
            meta[c, 1:2, :],
            jnp.where(lane < 2 * ROWS_Z, meta[c, 2:3, :], meta[c, 3:4, :]),
        )
        part = jnp.where(
            (lane % ROWS_Z == targets[c] % ROWS_Z) & (lane < 3 * ROWS_Z), part, 0.0
        )
        keys += dot_t(pick, part.astype(jnp.bfloat16))
    key_send[...] = keys.reshape(Z, 1, 128)
    key_z[0] = keys[0:1]
    for a in range(Z - 1, 0, -1):
        remote(
            key_send.at[a],
            key_z.at[a],
            key_send_sem.at[0],
            key_recv_sem.at[0],
            at(dz=z_offset(a)),
        )
    wait_bytes(key_z.at[pl.ds(1, Z - 1)], key_recv_sem.at[0])
    for d in range(1, Y):
        remote(key_z, key_y.at[d], key_send_sem.at[1], key_recv_sem.at[1], at(dy=d))
    key_y[0] = key_z[...]
    wait_bytes(key_y.at[pl.ds(1, Y - 1)], key_recv_sem.at[1])
    lane = iota((Z, 128), 1)
    merged = jnp.zeros((Z, 128), jnp.float32)
    for d in range(Y):
        merged += jnp.where(lane % ROWS_Z // BLOCK == d, key_y[d].reshape(Z, 128), 0.0)
    merged = (
        merged * 16384.0
        + pltpu.roll(merged, 128 - ROWS_Z, 1) * 128.0
        + pltpu.roll(merged, 128 - 2 * ROWS_Z, 1)
    )
    key_x[0] = jnp.where(merged == 0.0, EMPTY, merged)
    for place, dx in ((1, 1), (2, X - 1), (3, 2)):
        remote(
            key_x.at[0], key_x.at[place], key_send_sem.at[2], key_recv_sem.at[2], at(dx=dx)
        )

    def group(g):
        return pl.ds(g * GROUP, GROUP)

    def forward(g):
        wait_bytes(panels.at[1, group(g)], x1_recv.at[g])
        wait_bytes(panels.at[2, group(g)], x2_recv.at[g])
        held, dx = (1, 1) if g % 2 else (2, -1)
        remote(
            panels.at[held, group(g)], panels.at[3, group(g)], x_send, x3_recv.at[g], at(dx=dx)
        )

    for g in range(GROUPS - 1, -1, -1):
        low = max(g * GROUP, 1)
        wait_bytes(from_z.at[pl.ds(low, (g + 1) * GROUP - low)], z_recv.at[g])
        for d in range(1, Y):
            remote(
                from_z.at[group(g), d],
                panels.at[0, group(g), d],
                y_send,
                y_recv.at[g],
                at(dy=d),
            )
        pltpu.make_async_copy(
            from_z.at[group(g), 0], panels.at[0, group(g), 0], y_recv.at[g]
        ).start()
        wait_bytes(panels.at[0, group(g)], y_recv.at[g])
        remote(panels.at[0, group(g)], panels.at[1, group(g)], x_send, x1_recv.at[g], at(dx=1))
        remote(panels.at[0, group(g)], panels.at[2, group(g)], x_send, x2_recv.at[g], at(dx=-1))
        if g == GROUPS - 1:
            wait_bytes(key_x.at[pl.ds(1, X - 1)], key_recv_sem.at[2])
            shape = (Z, ROWS_Z, 128)
            for p in range(X):
                spread = jnp.broadcast_to(key_x[p].reshape(Z, 1, 128), shape)
                column = jnp.sum(
                    jnp.where(iota(shape, 2) == iota(shape, 1), spread, 0.0),
                    axis=2,
                    keepdims=True,
                )
                key_cols[p] = jnp.broadcast_to(column, shape).reshape(PANEL, 128)
        else:
            forward(g + 1)
    forward(0)
    for g in range(GROUPS - 1, -1, -1):
        wait_bytes(panels.at[3, group(g)], x3_recv.at[g])

    width = units.shape[2]
    own_keys = jnp.transpose(key_cols[0])[0:1, :]
    half = Z // 2

    def tile(step, best):
        p, h = step // 2, step % 2
        own = panels[0].reshape(PANEL, width)
        others = panels[p, pl.ds(h * half, half)].reshape(half * ROWS_Z, width)
        scores = dot_t(others, own)
        other_keys = key_cols[p, pl.ds(h * half * ROWS_Z, half * ROWS_Z), :][:, 0:1]
        scores = jnp.where(other_keys < own_keys, scores, -1.0)
        return jnp.maximum(best, jnp.max(scores, axis=0, keepdims=True))

    best = lax.fori_loop(0, 2 * X, tile, jnp.full((1, PANEL), -1.0, jnp.float32))

    for i in range(PANEL // 128):
        result[i] = best[:, i * 128 : (i + 1) * 128]
    for a in range(Z - 1, 0, -1):
        remote(
            result.at[a // 4],
            ret_z.at[a],
            ret_send_sem.at[0],
            ret_recv_sem.at[0],
            at(dz=-z_offset(a)),
        )
    ret_z[0] = result[0]
    wait_bytes(ret_z.at[pl.ds(1, Z - 1)], ret_recv_sem.at[0])
    for d in range(Y):
        for other in range(CORES):
            if d or other:
                remote(
                    ret_z,
                    ret_y.at[core * Y + d],
                    ret_send_sem.at[1],
                    ret_recv_sem.at[1],
                    at(dy=-d, dcore=other),
                )
    ret_y[core * Y] = ret_z[...]
    wait_bytes(ret_y.at[pl.ds(1, CORES * Y - 1)], ret_recv_sem.at[1])
    table = []
    for c in range(CORES):
        merged = jnp.zeros((Z, 128), jnp.float32)
        for d in range(Y):
            merged += jnp.where(lane % ROWS_Z // BLOCK == d, ret_y[c * Y + d].reshape(Z, 128), 0.0)
        table.append(merged)
    table = jnp.concatenate(table, axis=0)
    code = meta[core, 0:1, :].astype(jnp.int32)
    spot = code % PANEL
    chosen = (iota((128, rows), 0) == spot % 128).astype(jnp.float32)
    found = jnp.dot(
        table, chosen, precision=lax.Precision.HIGHEST, preferred_element_type=jnp.float32
    )
    wanted = code // PANEL * Z + spot // ROWS_Z
    found = jnp.where(iota((CORES * Z, rows), 0) == wanted, found, 0.0)
    out_ref[...] = jnp.sum(found, axis=0, keepdims=True)

    wait_bytes(units.at[0], core_send.at[0])
    wait_bytes(meta.at[0], core_send.at[1])
    wait_bytes(from_z.at[pl.ds(1, Z - 1)], z_send)
    wait_bytes(panels.at[0, pl.ds(0, Z * (Y - 1) // Y)], y_send)
    wait_bytes(panels.at[pl.ds(1, X - 1)], x_send)
    wait_bytes(key_z.at[pl.ds(1, Z - 1)], key_send_sem.at[0])
    wait_bytes(key_y.at[pl.ds(1, Y - 1)], key_send_sem.at[1])
    wait_bytes(key_x.at[pl.ds(1, X - 1)], key_send_sem.at[2])
    wait_bytes(ret_z.at[pl.ds(1, Z - 1)], ret_send_sem.at[0])
    wait_bytes(ret_y.at[pl.ds(1, CORES * Y - 1)], ret_send_sem.at[1])


def body(embeddings, cluster, order_rank):
    rows, width = embeddings.shape
    vmem = pl.BlockSpec(memory_space=pltpu.VMEM)
    dma = pltpu.SemaphoreType.DMA
    found = pl.pallas_call(
        kernel,
        out_shape=jax.ShapeDtypeStruct((1, rows), jnp.float32),
        in_specs=[vmem] * 3,
        out_specs=vmem,
        scratch_shapes=[
            pltpu.VMEM((CORES, rows, width), jnp.bfloat16),
            pltpu.VMEM((CORES, 8, rows), jnp.float32),
            pltpu.VMEM((Z, Y, BLOCK, width), jnp.bfloat16),
            pltpu.VMEM((Z, Y, BLOCK, width), jnp.bfloat16),
            pltpu.VMEM((X, Z, Y, BLOCK, width), jnp.bfloat16),
            pltpu.VMEM((Z, 1, 128), jnp.float32),
            pltpu.VMEM((Z, 1, 128), jnp.float32),
            pltpu.VMEM((Y, Z, 1, 128), jnp.float32),
            pltpu.VMEM((X, Z, 128), jnp.float32),
            pltpu.VMEM((X, PANEL, 128), jnp.float32),
            pltpu.VMEM((PANEL // 128, 1, 128), jnp.float32),
            pltpu.VMEM((Z, 1, 128), jnp.float32),
            pltpu.VMEM((CORES * Y, Z, 1, 128), jnp.float32),
            dma((2,)),
            dma((2,)),
            dma,
            dma((GROUPS,)),
            dma,
            dma((GROUPS,)),
            dma,
            dma((GROUPS,)),
            dma((GROUPS,)),
            dma((GROUPS,)),
            dma((3,)),
            dma((3,)),
            dma((2,)),
            dma((2,)),
        ],
        compiler_params=pltpu.CompilerParams(
            collective_id=0, has_side_effects=True, vmem_limit_bytes=48 * 1024 * 1024
        ),
    )(embeddings, cluster, order_rank)
    return found.reshape(rows)


def solution(mesh):
    return jax.shard_map(
        body,
        mesh=mesh,
        in_specs=(P(("dp", "helper"), None), P(("dp", "helper")), P(("dp", "helper"))),
        out_specs=P(("dp", "helper")),
        check_vma=False,
    )
```

```python
import functools

import jax
import jax.numpy as jnp
from jax import lax
from jax.experimental import pallas as pl
from jax.experimental.pallas import tpu as pltpu
from jax.sharding import PartitionSpec as P

MESH = pl.DeviceIdType.MESH
Y, Z, CORES, X = 4, 16, 2, 4
SLOTS = 4
BLOCK = CORES * SLOTS
ROWS_Z = Y * BLOCK
PANEL = Z * ROWS_Z
SPANS = tuple((low, low + 2) for low in range(0, Z, 2))
GROUPS = len(SPANS)
PACE = (-1,) * GROUPS
KEY_STEP = 2
LAG_X = 1
HELD = 3
EMPTY = 8388608.0


def z_offset(index):
    return (index + 1) // 2 if index % 2 else -(index // 2)


def wait_bytes(ref, sem):
    pltpu.make_async_copy(ref, ref, sem).wait()


def iota(shape, dim):
    return lax.broadcasted_iota(jnp.int32, shape, dim)


def dot_t(lhs, rhs):
    return lax.dot_general(lhs, rhs, (((1,), (1,)), ((), ())), preferred_element_type=jnp.float32)


def kernel(
    emb_hbm,
    cluster_hbm,
    rank_hbm,
    out_ref,
    emb_ref,
    cluster_ref,
    rank_ref,
    units,
    send_z,
    from_z,
    landed,
    panels,
    key_send,
    key_z,
    key_y,
    key_x,
    key_cols,
    result,
    ret_z,
    ret_y,
    z_send,
    z_recv,
    y_send,
    y_recv,
    x_send,
    x1_recv,
    x2_recv,
    key_send_sem,
    key_recv_sem,
    ret_send_sem,
    ret_recv_sem,
    load_sem,
    far_send,
    far_recv,
    far_sem,
):
    dp, hx = lax.axis_index("dp"), lax.axis_index("helper")
    core, chip = dp % CORES, dp // CORES
    y, z = chip // Z, chip % Z

    def at(dy=0, dz=0, dx=0, dcore=0):
        chip_to = ((y + dy + Y) % Y) * Z + (z + dz + Z) % Z
        return (chip_to * CORES + (core + dcore) % CORES, (hx + dx + X) % X)

    def remote(src, dst, send_sem, recv_sem, to):
        pltpu.make_async_remote_copy(
            src_ref=src,
            dst_ref=dst,
            send_sem=send_sem,
            recv_sem=recv_sem,
            device_id=to,
            device_id_type=MESH,
        ).start()

    loads = [
        pltpu.make_async_copy(src, dst, load_sem.at[i])
        for i, (src, dst) in enumerate(
            ((cluster_hbm, cluster_ref), (rank_hbm, rank_ref), (emb_hbm, emb_ref))
        )
    ]
    for load in loads:
        load.start()
    barrier = pltpu.get_barrier_semaphore()
    peers = [at(dz=z_offset(a)) for a in range(Z - 1, 0, -1)]
    peers += [at(dy=d) for d in range(1, Y)] + [at(dy=d, dcore=1) for d in range(Y)]
    peers += [at(dx=1), at(dx=-1)]
    for peer in peers:
        pl.semaphore_signal(barrier, inc=1, device_id=peer, device_id_type=MESH)

    rows, width = emb_ref.shape
    loads[0].wait()
    loads[1].wait()
    cluster = cluster_ref[...].reshape(1, rows)
    rank = rank_ref[...].reshape(1, rows)
    across = jnp.broadcast_to(cluster, (rows, rows))
    down = jnp.transpose(across)
    same_before = (down == across) & (iota((rows, rows), 0) < iota((rows, rows), 1))
    slot = jnp.sum(same_before.astype(jnp.float32), axis=0, keepdims=True).astype(jnp.int32)
    owner_core, owner_chip = cluster % CORES, cluster // CORES
    dy = (owner_chip // Z - y + Y) % Y
    dz = (owner_chip % Z - z + Z) % Z
    a_of = jnp.where(dz == 0, 0, jnp.where(dz <= Z // 2, 2 * dz - 1, 2 * (Z - dz)))
    place = (owner_core * Y + dy) * SLOTS + slot
    target = a_of * ROWS_Z + place

    loads[2].wait()
    values = emb_ref[...].astype(jnp.float32)
    scale = lax.rsqrt(jnp.sum(values * values, axis=-1, keepdims=True) + 1e-06)
    units[...] = (values * scale).astype(jnp.bfloat16)
    chunk = 4 * ROWS_Z
    for first in range(0, Z, 4):
        pick = (iota((chunk, rows), 0) + first * ROWS_Z == target).astype(jnp.float32)
        picked = jnp.dot(
            pick.astype(jnp.bfloat16), units[...], preferred_element_type=jnp.float32
        )
        picked = picked.astype(jnp.bfloat16).reshape(4, CORES, Y, SLOTS, width)
        for i in range(4):
            if first + i:
                send_z[first + i] = picked[i]
            else:
                from_z[0] = picked[0]

    def group_of(a):
        return next(g for g, (low, high) in enumerate(SPANS) if low <= a < high)

    def release(arrived):
        for g, (low, high) in enumerate(SPANS):
            if PACE[g] == arrived:
                for a in range(max(low, 1), high):
                    send_rows(a)

    def send_rows(a):
        remote(
            send_z.at[a], from_z.at[a], z_send, z_recv.at[group_of(a)], at(dz=z_offset(a))
        )

    key = rank * (Z * Y * CORES * X * SLOTS) + (dp * X + hx) * SLOTS + slot + 1
    parts = [key // 16384, key // 128 % 128, key % 128]
    lane = iota((128, rows), 0)
    spread = jnp.where(
        lane < ROWS_Z, parts[0], jnp.where(lane < 2 * ROWS_Z, parts[1], parts[2])
    )
    spread = jnp.where((lane % ROWS_Z == place) & (lane < 3 * ROWS_Z), spread, 0)
    pick = (iota((Z, rows), 0) == a_of).astype(jnp.float32).astype(jnp.bfloat16)
    keys = dot_t(pick, spread.astype(jnp.float32).astype(jnp.bfloat16))
    key_send[...] = keys.reshape(Z, 1, 128)
    key_z[0] = keys[0:1]
    pl.semaphore_wait(barrier, len(peers))
    for a in range(1, Z):
        remote(
            key_send.at[a],
            key_z.at[a],
            key_send_sem.at[0],
            key_recv_sem.at[0],
            at(dz=z_offset(a)),
        )
    release(-1)
    lane = iota((Z, 128), 1)

    def keys_to_y():
        wait_bytes(key_z.at[pl.ds(1, Z - 1)], key_recv_sem.at[0])
        for d in range(Y):
            for other in range(CORES):
                if d or other:
                    remote(
                        key_z,
                        key_y.at[core * Y + d],
                        key_send_sem.at[1],
                        key_recv_sem.at[1],
                        at(dy=d, dcore=other),
                    )
        key_y[core * Y] = key_z[...]

    def keys_to_x():
        wait_bytes(key_y.at[pl.ds(1, CORES * Y - 1)], key_recv_sem.at[1])
        merged = jnp.zeros((Z, 128), jnp.float32)
        for c in range(CORES):
            for d in range(Y):
                shift = (128 + SLOTS * (d + c) - Y * SLOTS * core) % 128
                moved = pltpu.roll(key_y[c * Y + d].reshape(Z, 128), shift, 1)
                merged += jnp.where(lane % ROWS_Z // SLOTS == CORES * d + c, moved, 0.0)
        merged = (
            merged * 16384.0
            + pltpu.roll(merged, 128 - ROWS_Z, 1) * 128.0
            + pltpu.roll(merged, 128 - 2 * ROWS_Z, 1)
        )
        key_x[0] = jnp.where(merged == 0.0, EMPTY, merged)
        for place, dx in ((1, 1), (2, -1)):
            remote(
                key_x.at[0], key_x.at[place], key_send_sem.at[2], key_recv_sem.at[2], at(dx=dx)
            )

    def group(g):
        return pl.ds(SPANS[g][0], SPANS[g][1] - SPANS[g][0])

    def to_y(g):
        low, high = SPANS[g]
        low = max(low, 1)
        wait_bytes(from_z.at[pl.ds(low, high - low)], z_recv.at[g])
        release(g)
        for d in range(Y):
            for other in range(CORES):
                src = from_z.at[group(g), (core + other) % CORES, d]
                dst = landed.at[group(g), d, core]
                if d or other:
                    remote(src, dst, y_send, y_recv.at[g], at(dy=d, dcore=other))
                else:
                    pltpu.make_async_copy(src, dst, y_recv.at[g]).start()

    def to_x(g):
        wait_bytes(landed.at[group(g)], y_recv.at[g])
        panels[0, group(g)] = landed[group(g)].reshape(-1, Y, BLOCK, width)
        remote(panels.at[0, group(g)], panels.at[1, group(g)], x_send, x1_recv.at[g], at(dx=1))
        remote(panels.at[0, group(g)], panels.at[2, group(g)], x_send, x2_recv.at[g], at(dx=-1))

    def key_columns():
        wait_bytes(key_x.at[pl.ds(1, HELD - 1)], key_recv_sem.at[2])
        shape = (Z, ROWS_Z, 128)
        for p in range(HELD):
            spread = jnp.broadcast_to(key_x[p].reshape(Z, 1, 128), shape)
            column = jnp.sum(
                jnp.where(iota(shape, 2) == iota(shape, 1), spread, 0.0),
                axis=2,
                keepdims=True,
            )
            key_cols[p] = jnp.broadcast_to(column, shape).reshape(PANEL, 128)

    key_steps = {KEY_STEP: keys_to_y, KEY_STEP + 1: keys_to_x, KEY_STEP + 2: key_columns}
    for step in range(GROUPS + LAG_X):
        if step < GROUPS:
            to_y(step)
        if step >= LAG_X:
            to_x(step - LAG_X)
        if step in key_steps:
            key_steps[step]()

    half = Z // 2

    def arrived(low, high):
        for g, (first, last) in enumerate(SPANS):
            if low <= first < high:
                wait_bytes(panels.at[1, group(g)], x1_recv.at[g])
                wait_bytes(panels.at[2, group(g)], x2_recv.at[g])

    def largest(query, best, tiles):
        query_keys = jnp.transpose(key_cols[query])[0:1, :]

        def tile(step, best):
            p, h = tiles(step)
            queries = panels[query].reshape(PANEL, width)
            others = panels[p, pl.ds(h * half, half)].reshape(half * ROWS_Z, width)
            scores = dot_t(others, queries)
            other_keys = key_cols[p, pl.ds(h * half * ROWS_Z, half * ROWS_Z), :][:, 0:1]
            scores = jnp.where(other_keys < query_keys, scores, -1.0)
            return jnp.maximum(best, jnp.max(scores, axis=0, keepdims=True))

        return lambda count: lax.fori_loop(0, count, tile, best)

    none = jnp.full((1, PANEL), -1.0, jnp.float32)
    best = largest(0, none, lambda step: (0, step))(2)
    arrived(0, half)
    best = largest(0, best, lambda step: (1 + step, 0))(2)
    arrived(half, Z)
    far = largest(1, none, lambda step: (2, step))(2)
    for i in range(PANEL // 128):
        far_send[i] = far[:, i * 128 : (i + 1) * 128]
    remote(far_send, far_recv, far_sem.at[0], far_sem.at[1], at(dx=-1))
    best = largest(0, best, lambda step: (1 + step, 1))(2)
    wait_bytes(far_recv, far_sem.at[1])

    for i in range(PANEL // 128):
        result[i] = jnp.maximum(best[:, i * 128 : (i + 1) * 128], far_recv[i])
    for a in range(Z - 1, 0, -1):
        remote(
            result.at[a // 4],
            ret_z.at[a],
            ret_send_sem.at[0],
            ret_recv_sem.at[0],
            at(dz=-z_offset(a)),
        )
    ret_z[0] = result[0]
    wait_bytes(ret_z.at[pl.ds(1, Z - 1)], ret_recv_sem.at[0])
    for d in range(Y):
        for other in range(CORES):
            if d or other:
                remote(
                    ret_z,
                    ret_y.at[core * Y + d],
                    ret_send_sem.at[1],
                    ret_recv_sem.at[1],
                    at(dy=-d, dcore=other),
                )
    ret_y[core * Y] = ret_z[...]
    wait_bytes(ret_y.at[pl.ds(1, CORES * Y - 1)], ret_recv_sem.at[1])
    table = []
    for c in range(CORES):
        merged = jnp.zeros((Z, 128), jnp.float32)
        for d in range(Y):
            merged += jnp.where(lane % ROWS_Z // BLOCK == d, ret_y[c * Y + d].reshape(Z, 128), 0.0)
        table.append(merged)
    table = jnp.concatenate(table, axis=0)
    spot = a_of * ROWS_Z + dy * BLOCK + core * SLOTS + slot
    chosen = (iota((128, rows), 0) == spot % 128).astype(jnp.float32)
    found = jnp.dot(
        table, chosen, precision=lax.Precision.HIGHEST, preferred_element_type=jnp.float32
    )
    wanted = owner_core * Z + a_of
    found = jnp.where(iota((CORES * Z, rows), 0) == wanted, found, 0.0)
    out_ref[...] = jnp.sum(found, axis=0, keepdims=True)

    wait_bytes(from_z.at[pl.ds(1, Z - 1)], z_send)
    wait_bytes(landed.at[pl.ds(0, Z - Z // (Y * CORES))], y_send)
    wait_bytes(panels.at[pl.ds(1, HELD - 1)], x_send)
    wait_bytes(far_send, far_sem.at[0])
    wait_bytes(key_z.at[pl.ds(1, Z - 1)], key_send_sem.at[0])
    wait_bytes(key_y.at[pl.ds(1, CORES * Y - 1)], key_send_sem.at[1])
    wait_bytes(key_x.at[pl.ds(1, HELD - 1)], key_send_sem.at[2])
    wait_bytes(ret_z.at[pl.ds(1, Z - 1)], ret_send_sem.at[0])
    wait_bytes(ret_y.at[pl.ds(1, CORES * Y - 1)], ret_send_sem.at[1])


def body(embeddings, cluster, order_rank):
    rows, width = embeddings.shape
    vmem = pl.BlockSpec(memory_space=pltpu.VMEM)
    dma = pltpu.SemaphoreType.DMA
    found = pl.pallas_call(
        kernel,
        out_shape=jax.ShapeDtypeStruct((1, rows), jnp.float32),
        in_specs=[pl.BlockSpec(memory_space=pl.ANY)] * 3,
        out_specs=vmem,
        scratch_shapes=[
            pltpu.VMEM((rows, width), jnp.bfloat16),
            pltpu.VMEM((rows,), jnp.int32),
            pltpu.VMEM((rows,), jnp.int32),
            pltpu.VMEM((rows, width), jnp.bfloat16),
            pltpu.VMEM((Z, CORES, Y, SLOTS, width), jnp.bfloat16),
            pltpu.VMEM((Z, CORES, Y, SLOTS, width), jnp.bfloat16),
            pltpu.VMEM((Z, Y, CORES, SLOTS, width), jnp.bfloat16),
            pltpu.VMEM((HELD, Z, Y, BLOCK, width), jnp.bfloat16),
            pltpu.VMEM((Z, 1, 128), jnp.float32),
            pltpu.VMEM((Z, 1, 128), jnp.float32),
            pltpu.VMEM((CORES * Y, Z, 1, 128), jnp.float32),
            pltpu.VMEM((HELD, Z, 128), jnp.float32),
            pltpu.VMEM((HELD, PANEL, 128), jnp.float32),
            pltpu.VMEM((PANEL // 128, 1, 128), jnp.float32),
            pltpu.VMEM((Z, 1, 128), jnp.float32),
            pltpu.VMEM((CORES * Y, Z, 1, 128), jnp.float32),
            dma,
            dma((GROUPS,)),
            dma,
            dma((GROUPS,)),
            dma,
            dma((GROUPS,)),
            dma((GROUPS,)),
            dma((3,)),
            dma((3,)),
            dma((2,)),
            dma((2,)),
            dma((3,)),
            pltpu.VMEM((PANEL // 128, 1, 128), jnp.float32),
            pltpu.VMEM((PANEL // 128, 1, 128), jnp.float32),
            dma((2,)),
        ],
        compiler_params=pltpu.CompilerParams(
            collective_id=0, has_side_effects=True, vmem_limit_bytes=48 * 1024 * 1024
        ),
    )(embeddings, cluster, order_rank)
    return found.reshape(rows)


def solution(mesh):
    return jax.shard_map(
        body,
        mesh=mesh,
        in_specs=(P(("dp", "helper"), None), P(("dp", "helper")), P(("dp", "helper"))),
        out_specs=P(("dp", "helper")),
        check_vma=False,
    )
```

```python
import functools

import jax
import jax.numpy as jnp
from jax import lax
from jax.experimental import pallas as pl
from jax.experimental.pallas import tpu as pltpu
from jax.sharding import PartitionSpec as P

MESH = pl.DeviceIdType.MESH
Y, Z, CORES, X = 4, 16, 2, 4
SLOTS = 4
BLOCK = CORES * SLOTS
ROWS_Z = Y * BLOCK
PANEL = Z * ROWS_Z
SPANS = tuple((low, low + 2) for low in range(0, Z, 2))
GROUPS = len(SPANS)
PACE = (-1,) * GROUPS
KEY_STEP = 2
LAG_X = 1
HELD = 3
EMPTY = 8388608.0


def z_offset(index):
    return (index + 1) // 2 if index % 2 else -(index // 2)


def wait_bytes(ref, sem):
    pltpu.make_async_copy(ref, ref, sem).wait()


def iota(shape, dim):
    return lax.broadcasted_iota(jnp.int32, shape, dim)


def dot_t(lhs, rhs):
    return lax.dot_general(lhs, rhs, (((1,), (1,)), ((), ())), preferred_element_type=jnp.float32)


def kernel(
    emb_hbm,
    cluster_hbm,
    rank_hbm,
    out_ref,
    emb_ref,
    cluster_ref,
    rank_ref,
    units,
    send_z,
    from_z,
    landed,
    panels,
    key_send,
    key_z,
    key_y,
    key_x,
    key_cols,
    key_rows,
    result,
    ret_z,
    ret_y,
    z_send,
    z_recv,
    y_send,
    y_recv,
    x_send,
    x1_recv,
    x2_recv,
    key_send_sem,
    key_recv_sem,
    ret_send_sem,
    ret_recv_sem,
    load_sem,
    far_send,
    far_recv,
    far_sem,
):
    dp, hx = lax.axis_index("dp"), lax.axis_index("helper")
    core, chip = dp % CORES, dp // CORES
    y, z = chip // Z, chip % Z

    def at(dy=0, dz=0, dx=0, dcore=0):
        chip_to = ((y + dy + Y) % Y) * Z + (z + dz + Z) % Z
        return (chip_to * CORES + (core + dcore) % CORES, (hx + dx + X) % X)

    def remote(src, dst, send_sem, recv_sem, to):
        pltpu.make_async_remote_copy(
            src_ref=src,
            dst_ref=dst,
            send_sem=send_sem,
            recv_sem=recv_sem,
            device_id=to,
            device_id_type=MESH,
        ).start()

    loads = [
        pltpu.make_async_copy(src, dst, load_sem.at[i])
        for i, (src, dst) in enumerate(
            ((cluster_hbm, cluster_ref), (rank_hbm, rank_ref), (emb_hbm, emb_ref))
        )
    ]
    for load in loads:
        load.start()
    barrier = pltpu.get_barrier_semaphore()
    peers = [at(dz=z_offset(a)) for a in range(Z - 1, 0, -1)]
    peers += [at(dy=d) for d in range(1, Y)] + [at(dy=d, dcore=1) for d in range(Y)]
    peers += [at(dx=1), at(dx=-1)]
    for peer in peers:
        pl.semaphore_signal(barrier, inc=1, device_id=peer, device_id_type=MESH)

    rows, width = emb_ref.shape
    loads[0].wait()
    loads[1].wait()
    cluster = cluster_ref[...].reshape(1, rows)
    rank = rank_ref[...].reshape(1, rows)
    across = jnp.broadcast_to(cluster, (rows, rows))
    down = jnp.transpose(across)
    same_before = (down == across) & (iota((rows, rows), 0) < iota((rows, rows), 1))
    slot = jnp.sum(same_before.astype(jnp.float32), axis=0, keepdims=True).astype(jnp.int32)
    owner_core, owner_chip = cluster % CORES, cluster // CORES
    dy = (owner_chip // Z - y + Y) % Y
    dz = (owner_chip % Z - z + Z) % Z
    a_of = jnp.where(dz == 0, 0, jnp.where(dz <= Z // 2, 2 * dz - 1, 2 * (Z - dz)))
    place = (owner_core * Y + dy) * SLOTS + slot
    target = a_of * ROWS_Z + place

    loads[2].wait()
    values = emb_ref[...].astype(jnp.float32)
    scale = lax.rsqrt(jnp.sum(values * values, axis=-1, keepdims=True) + 1e-06)
    units[...] = (values * scale).astype(jnp.bfloat16)
    chunk = 4 * ROWS_Z
    for first in range(0, Z, 4):
        pick = (iota((chunk, rows), 0) + first * ROWS_Z == target).astype(jnp.float32)
        picked = jnp.dot(
            pick.astype(jnp.bfloat16), units[...], preferred_element_type=jnp.float32
        )
        picked = picked.astype(jnp.bfloat16).reshape(4, CORES, Y, SLOTS, width)
        for i in range(4):
            if first + i:
                send_z[first + i] = picked[i]
            else:
                from_z[0] = picked[0]

    def group_of(a):
        return next(g for g, (low, high) in enumerate(SPANS) if low <= a < high)

    def release(arrived):
        for g, (low, high) in enumerate(SPANS):
            if PACE[g] == arrived:
                for a in range(max(low, 1), high):
                    send_rows(a)

    def send_rows(a):
        remote(
            send_z.at[a], from_z.at[a], z_send, z_recv.at[group_of(a)], at(dz=z_offset(a))
        )

    key = rank * (Z * Y * CORES * X * SLOTS) + (dp * X + hx) * SLOTS + slot + 1
    parts = [key // 16384, key // 128 % 128, key % 128]
    lane = iota((128, rows), 0)
    spread = jnp.where(
        lane < ROWS_Z, parts[0], jnp.where(lane < 2 * ROWS_Z, parts[1], parts[2])
    )
    spread = jnp.where((lane % ROWS_Z == place) & (lane < 3 * ROWS_Z), spread, 0)
    pick = (iota((Z, rows), 0) == a_of).astype(jnp.float32).astype(jnp.bfloat16)
    keys = dot_t(pick, spread.astype(jnp.float32).astype(jnp.bfloat16))
    key_send[...] = keys.reshape(Z, 1, 128)
    key_z[0] = keys[0:1]
    pl.semaphore_wait(barrier, len(peers))
    for a in range(1, Z):
        remote(
            key_send.at[a],
            key_z.at[a],
            key_send_sem.at[0],
            key_recv_sem.at[0],
            at(dz=z_offset(a)),
        )
    release(-1)
    lane = iota((Z, 128), 1)

    def keys_to_y():
        wait_bytes(key_z.at[pl.ds(1, Z - 1)], key_recv_sem.at[0])
        for d in range(Y):
            for other in range(CORES):
                if d or other:
                    remote(
                        key_z,
                        key_y.at[core * Y + d],
                        key_send_sem.at[1],
                        key_recv_sem.at[1],
                        at(dy=d, dcore=other),
                    )
        key_y[core * Y] = key_z[...]

    def keys_to_x():
        wait_bytes(key_y.at[pl.ds(1, CORES * Y - 1)], key_recv_sem.at[1])
        merged = jnp.zeros((Z, 128), jnp.float32)
        for c in range(CORES):
            for d in range(Y):
                shift = (128 + SLOTS * (d + c) - Y * SLOTS * core) % 128
                moved = pltpu.roll(key_y[c * Y + d].reshape(Z, 128), shift, 1)
                merged += jnp.where(lane % ROWS_Z // SLOTS == CORES * d + c, moved, 0.0)
        merged = (
            merged * 16384.0
            + pltpu.roll(merged, 128 - ROWS_Z, 1) * 128.0
            + pltpu.roll(merged, 128 - 2 * ROWS_Z, 1)
        )
        key_x[0] = jnp.where(merged == 0.0, EMPTY, merged)
        for place, dx in ((1, 1), (2, -1)):
            remote(
                key_x.at[0], key_x.at[place], key_send_sem.at[2], key_recv_sem.at[2], at(dx=dx)
            )

    def group(g):
        return pl.ds(SPANS[g][0], SPANS[g][1] - SPANS[g][0])

    def lines(g):
        return pl.ds(SPANS[g][0] * ROWS_Z, (SPANS[g][1] - SPANS[g][0]) * ROWS_Z)

    def to_y(g):
        low, high = SPANS[g]
        low = max(low, 1)
        wait_bytes(from_z.at[pl.ds(low, high - low)], z_recv.at[g])
        release(g)
        for d in range(Y):
            for other in range(CORES):
                src = from_z.at[group(g), (core + other) % CORES, d]
                dst = landed.at[group(g), d, core]
                if d or other:
                    remote(src, dst, y_send, y_recv.at[g], at(dy=d, dcore=other))
                else:
                    pltpu.make_async_copy(src, dst, y_recv.at[g]).start()

    def to_x(g):
        wait_bytes(landed.at[group(g)], y_recv.at[g])
        panels[0, lines(g)] = landed[group(g)].reshape(-1, width)
        remote(panels.at[0, lines(g)], panels.at[1, lines(g)], x_send, x1_recv.at[g], at(dx=1))
        remote(panels.at[0, lines(g)], panels.at[2, lines(g)], x_send, x2_recv.at[g], at(dx=-1))

    def key_columns():
        wait_bytes(key_x.at[pl.ds(1, HELD - 1)], key_recv_sem.at[2])
        shape = (Z, ROWS_Z, 128)
        for p in range(HELD):
            spread = jnp.broadcast_to(key_x[p].reshape(Z, 1, 128), shape)
            column = jnp.sum(
                jnp.where(iota(shape, 2) == iota(shape, 1), spread, 0.0),
                axis=2,
                keepdims=True,
            )
            key_cols[p] = jnp.broadcast_to(column, shape).reshape(PANEL, 128)
        for p in range(HELD - 1):
            key_rows[p] = jnp.transpose(key_cols[p])[0:1, :]

    key_steps = {KEY_STEP: keys_to_y, KEY_STEP + 1: keys_to_x, KEY_STEP + 2: key_columns}
    for step in range(GROUPS + LAG_X):
        if step < GROUPS:
            to_y(step)
        if step >= LAG_X:
            to_x(step - LAG_X)
        if step in key_steps:
            key_steps[step]()

    half = Z // 2

    def arrived(low, high):
        for g, (first, last) in enumerate(SPANS):
            if low <= first < high:
                wait_bytes(panels.at[1, lines(g)], x1_recv.at[g])
                wait_bytes(panels.at[2, lines(g)], x2_recv.at[g])

    def largest(query, best, tiles):
        def tile(step, best):
            p, h = tiles(step)
            at_rows = pl.ds(h * half * ROWS_Z, half * ROWS_Z)
            scores = dot_t(panels[p, at_rows, :], panels[query])
            earlier = key_cols[p, at_rows, :][:, 0:1] < key_rows[query]
            scores = jnp.where(earlier, scores, -1.0)
            return jnp.maximum(best, jnp.max(scores, axis=0, keepdims=True))

        return lambda count: lax.fori_loop(0, count, tile, best)

    none = jnp.full((1, PANEL), -1.0, jnp.float32)
    best = largest(0, none, lambda step: (0, step))(2)
    arrived(0, half)
    best = largest(0, best, lambda step: (1 + step, 0))(2)
    arrived(half, Z)
    far = largest(1, none, lambda step: (2, step))(2)
    for i in range(PANEL // 128):
        far_send[i] = far[:, i * 128 : (i + 1) * 128]
    remote(far_send, far_recv, far_sem.at[0], far_sem.at[1], at(dx=-1))
    best = largest(0, best, lambda step: (1 + step, 1))(2)
    wait_bytes(far_recv, far_sem.at[1])

    for i in range(PANEL // 128):
        result[i] = jnp.maximum(best[:, i * 128 : (i + 1) * 128], far_recv[i])
    for a in range(Z - 1, 0, -1):
        remote(
            result.at[a // 4],
            ret_z.at[a],
            ret_send_sem.at[0],
            ret_recv_sem.at[0],
            at(dz=-z_offset(a)),
        )
    spot = a_of * ROWS_Z + dy * BLOCK + core * SLOTS + slot
    chosen = (iota((128, rows), 0) == spot % 128).astype(jnp.float32)
    wanted = iota((CORES * Z, rows), 0) == owner_core * Z + a_of
    ret_z[0] = result[0]
    wait_bytes(ret_z.at[pl.ds(1, Z - 1)], ret_recv_sem.at[0])
    for d in range(Y):
        for other in range(CORES):
            if d or other:
                remote(
                    ret_z,
                    ret_y.at[core * Y + d],
                    ret_send_sem.at[1],
                    ret_recv_sem.at[1],
                    at(dy=-d, dcore=other),
                )
    ret_y[core * Y] = ret_z[...]
    wait_bytes(ret_y.at[pl.ds(1, CORES * Y - 1)], ret_recv_sem.at[1])
    table = []
    for c in range(CORES):
        merged = jnp.zeros((Z, 128), jnp.float32)
        for d in range(Y):
            merged += jnp.where(lane % ROWS_Z // BLOCK == d, ret_y[c * Y + d].reshape(Z, 128), 0.0)
        table.append(merged)
    table = jnp.concatenate(table, axis=0)
    found = jnp.dot(
        table, chosen, precision=lax.Precision.HIGHEST, preferred_element_type=jnp.float32
    )
    found = jnp.where(wanted, found, 0.0)
    out_ref[...] = jnp.sum(found, axis=0, keepdims=True)

    wait_bytes(from_z.at[pl.ds(1, Z - 1)], z_send)
    wait_bytes(landed.at[pl.ds(0, Z - Z // (Y * CORES))], y_send)
    wait_bytes(panels.at[pl.ds(1, HELD - 1)], x_send)
    wait_bytes(far_send, far_sem.at[0])
    wait_bytes(key_z.at[pl.ds(1, Z - 1)], key_send_sem.at[0])
    wait_bytes(key_y.at[pl.ds(1, CORES * Y - 1)], key_send_sem.at[1])
    wait_bytes(key_x.at[pl.ds(1, HELD - 1)], key_send_sem.at[2])
    wait_bytes(ret_z.at[pl.ds(1, Z - 1)], ret_send_sem.at[0])
    wait_bytes(ret_y.at[pl.ds(1, CORES * Y - 1)], ret_send_sem.at[1])


def body(embeddings, cluster, order_rank):
    rows, width = embeddings.shape
    vmem = pl.BlockSpec(memory_space=pltpu.VMEM)
    dma = pltpu.SemaphoreType.DMA
    found = pl.pallas_call(
        kernel,
        out_shape=jax.ShapeDtypeStruct((1, rows), jnp.float32),
        in_specs=[pl.BlockSpec(memory_space=pl.ANY)] * 3,
        out_specs=vmem,
        scratch_shapes=[
            pltpu.VMEM((rows, width), jnp.bfloat16),
            pltpu.VMEM((rows,), jnp.int32),
            pltpu.VMEM((rows,), jnp.int32),
            pltpu.VMEM((rows, width), jnp.bfloat16),
            pltpu.VMEM((Z, CORES, Y, SLOTS, width), jnp.bfloat16),
            pltpu.VMEM((Z, CORES, Y, SLOTS, width), jnp.bfloat16),
            pltpu.VMEM((Z, Y, CORES, SLOTS, width), jnp.bfloat16),
            pltpu.VMEM((HELD, PANEL, width), jnp.bfloat16),
            pltpu.VMEM((Z, 1, 128), jnp.float32),
            pltpu.VMEM((Z, 1, 128), jnp.float32),
            pltpu.VMEM((CORES * Y, Z, 1, 128), jnp.float32),
            pltpu.VMEM((HELD, Z, 128), jnp.float32),
            pltpu.VMEM((HELD, PANEL, 128), jnp.float32),
            pltpu.VMEM((HELD - 1, 1, PANEL), jnp.float32),
            pltpu.VMEM((PANEL // 128, 1, 128), jnp.float32),
            pltpu.VMEM((Z, 1, 128), jnp.float32),
            pltpu.VMEM((CORES * Y, Z, 1, 128), jnp.float32),
            dma,
            dma((GROUPS,)),
            dma,
            dma((GROUPS,)),
            dma,
            dma((GROUPS,)),
            dma((GROUPS,)),
            dma((3,)),
            dma((3,)),
            dma((2,)),
            dma((2,)),
            dma((3,)),
            pltpu.VMEM((PANEL // 128, 1, 128), jnp.float32),
            pltpu.VMEM((PANEL // 128, 1, 128), jnp.float32),
            dma((2,)),
        ],
        compiler_params=pltpu.CompilerParams(
            collective_id=0, has_side_effects=True, vmem_limit_bytes=60 * 1024 * 1024
        ),
    )(embeddings, cluster, order_rank)
    return found.reshape(rows)


def solution(mesh):
    return jax.shard_map(
        body,
        mesh=mesh,
        in_specs=(P(("dp", "helper"), None), P(("dp", "helper")), P(("dp", "helper"))),
        out_specs=P(("dp", "helper")),
        check_vma=False,
    )
```

```python
import functools

import jax
import jax.numpy as jnp
from jax import lax
from jax.experimental import pallas as pl
from jax.experimental.pallas import tpu as pltpu
from jax.sharding import PartitionSpec as P

MESH = pl.DeviceIdType.MESH
Y, Z, CORES, X = 4, 16, 2, 4
SLOTS = 4
BLOCK = CORES * SLOTS
ROWS_Z = Y * BLOCK
PANEL = Z * ROWS_Z
SPANS = tuple((low, low + 2) for low in range(0, Z, 2))
GROUPS = len(SPANS)
NEAR = 8
KEY_STEP = 2
LAG_X = 1
HELD = 3
EMPTY = 8388608.0


def z_offset(index):
    return (index + 1) // 2 if index % 2 else -(index // 2)


def wait_bytes(ref, sem):
    pltpu.make_async_copy(ref, ref, sem).wait()


def iota(shape, dim):
    return lax.broadcasted_iota(jnp.int32, shape, dim)


def dot_t(lhs, rhs):
    return lax.dot_general(lhs, rhs, (((1,), (1,)), ((), ())), preferred_element_type=jnp.float32)


def kernel(
    emb_hbm,
    cluster_hbm,
    rank_hbm,
    out_ref,
    emb_ref,
    cluster_ref,
    rank_ref,
    units,
    send_z,
    from_z,
    landed,
    panels,
    key_send,
    key_z,
    key_y,
    key_x,
    key_cols,
    key_rows,
    result,
    ret_z,
    ret_y,
    z_send,
    z_recv,
    y_send,
    y_recv,
    x_send,
    x1_recv,
    x2_recv,
    key_send_sem,
    key_recv_sem,
    ret_send_sem,
    ret_recv_sem,
    load_sem,
    far_send,
    far_recv,
    far_sem,
    all_in,
):
    dp, hx = lax.axis_index("dp"), lax.axis_index("helper")
    core, chip = dp % CORES, dp // CORES
    y, z = chip // Z, chip % Z

    def at(dy=0, dz=0, dx=0, dcore=0):
        chip_to = ((y + dy + Y) % Y) * Z + (z + dz + Z) % Z
        return (chip_to * CORES + (core + dcore) % CORES, (hx + dx + X) % X)

    def remote(src, dst, send_sem, recv_sem, to):
        pltpu.make_async_remote_copy(
            src_ref=src,
            dst_ref=dst,
            send_sem=send_sem,
            recv_sem=recv_sem,
            device_id=to,
            device_id_type=MESH,
        ).start()

    loads = [
        pltpu.make_async_copy(src, dst, load_sem.at[i])
        for i, (src, dst) in enumerate(
            ((cluster_hbm, cluster_ref), (rank_hbm, rank_ref), (emb_hbm, emb_ref))
        )
    ]
    for load in loads:
        load.start()
    barrier = pltpu.get_barrier_semaphore()
    peers = [at(dz=z_offset(a)) for a in range(NEAR, 0, -1)]
    peers += [at(dy=d) for d in range(1, Y)] + [at(dy=d, dcore=1) for d in range(Y)]
    peers += [at(dx=1), at(dx=-1)]
    for peer in peers:
        pl.semaphore_signal(barrier, inc=1, device_id=peer, device_id_type=MESH)

    rows, width = emb_ref.shape
    loads[0].wait()
    loads[1].wait()
    cluster = cluster_ref[...].reshape(1, rows)
    rank = rank_ref[...].reshape(1, rows)
    across = jnp.broadcast_to(cluster, (rows, rows))
    down = jnp.transpose(across)
    same_before = (down == across) & (iota((rows, rows), 0) < iota((rows, rows), 1))
    slot = jnp.sum(same_before.astype(jnp.float32), axis=0, keepdims=True).astype(jnp.int32)
    owner_core, owner_chip = cluster % CORES, cluster // CORES
    dy = (owner_chip // Z - y + Y) % Y
    dz = (owner_chip % Z - z + Z) % Z
    a_of = jnp.where(dz == 0, 0, jnp.where(dz <= Z // 2, 2 * dz - 1, 2 * (Z - dz)))
    place = (owner_core * Y + dy) * SLOTS + slot
    target = a_of * ROWS_Z + place

    loads[2].wait()
    values = emb_ref[...].astype(jnp.float32)
    scale = lax.rsqrt(jnp.sum(values * values, axis=-1, keepdims=True) + 1e-06)
    units[...] = (values * scale).astype(jnp.bfloat16)
    chunk = 4 * ROWS_Z
    for first in range(0, Z, 4):
        pick = (iota((chunk, rows), 0) + first * ROWS_Z == target).astype(jnp.float32)
        picked = jnp.dot(
            pick.astype(jnp.bfloat16), units[...], preferred_element_type=jnp.float32
        )
        picked = picked.astype(jnp.bfloat16).reshape(4, CORES, Y, SLOTS, width)
        for i in range(4):
            if first + i:
                send_z[first + i] = picked[i]
            else:
                from_z[0] = picked[0]

    def group_of(a):
        return next(g for g, (low, high) in enumerate(SPANS) if low <= a < high)

    def release(first, last):
        for a in range(first, last):
            send_key(a)
        for a in range(first, last):
            send_rows(a)

    def send_key(a):
        remote(
            key_send.at[a],
            key_z.at[a],
            key_send_sem.at[0],
            key_recv_sem.at[0],
            at(dz=z_offset(a)),
        )

    def send_rows(a):
        remote(
            send_z.at[a], from_z.at[a], z_send, z_recv.at[group_of(a)], at(dz=z_offset(a))
        )

    key = rank * (Z * Y * CORES * X * SLOTS) + (dp * X + hx) * SLOTS + slot + 1
    parts = [key // 16384, key // 128 % 128, key % 128]
    lane = iota((128, rows), 0)
    spread = jnp.where(
        lane < ROWS_Z, parts[0], jnp.where(lane < 2 * ROWS_Z, parts[1], parts[2])
    )
    spread = jnp.where((lane % ROWS_Z == place) & (lane < 3 * ROWS_Z), spread, 0)
    pick = (iota((Z, rows), 0) == a_of).astype(jnp.float32).astype(jnp.bfloat16)
    keys = dot_t(pick, spread.astype(jnp.float32).astype(jnp.bfloat16))
    key_send[...] = keys.reshape(Z, 1, 128)
    key_z[0] = keys[0:1]
    pl.semaphore_wait(barrier, len(peers))
    for dz in (Z // 4, -(Z // 4)):
        pl.semaphore_signal(all_in, inc=1, device_id=at(dz=dz), device_id_type=MESH)
    release(1, NEAR + 1)
    pl.semaphore_wait(all_in, 2)
    release(NEAR + 1, Z)

    lane = iota((Z, 128), 1)

    def keys_to_y():
        wait_bytes(key_z.at[pl.ds(1, Z - 1)], key_recv_sem.at[0])
        for d in range(Y):
            for other in range(CORES):
                if d or other:
                    remote(
                        key_z,
                        key_y.at[core * Y + d],
                        key_send_sem.at[1],
                        key_recv_sem.at[1],
                        at(dy=d, dcore=other),
                    )
        key_y[core * Y] = key_z[...]

    def keys_to_x():
        wait_bytes(key_y.at[pl.ds(1, CORES * Y - 1)], key_recv_sem.at[1])
        merged = jnp.zeros((Z, 128), jnp.float32)
        for c in range(CORES):
            for d in range(Y):
                shift = (128 + SLOTS * (d + c) - Y * SLOTS * core) % 128
                moved = pltpu.roll(key_y[c * Y + d].reshape(Z, 128), shift, 1)
                merged += jnp.where(lane % ROWS_Z // SLOTS == CORES * d + c, moved, 0.0)
        merged = (
            merged * 16384.0
            + pltpu.roll(merged, 128 - ROWS_Z, 1) * 128.0
            + pltpu.roll(merged, 128 - 2 * ROWS_Z, 1)
        )
        key_x[0] = jnp.where(merged == 0.0, EMPTY, merged)
        for place, dx in ((1, 1), (2, -1)):
            remote(
                key_x.at[0], key_x.at[place], key_send_sem.at[2], key_recv_sem.at[2], at(dx=dx)
            )

    def group(g):
        return pl.ds(SPANS[g][0], SPANS[g][1] - SPANS[g][0])

    def lines(g):
        return pl.ds(SPANS[g][0] * ROWS_Z, (SPANS[g][1] - SPANS[g][0]) * ROWS_Z)

    def to_y(g):
        low, high = SPANS[g]
        low = max(low, 1)
        wait_bytes(from_z.at[pl.ds(low, high - low)], z_recv.at[g])
        for d in range(Y):
            for other in range(CORES):
                src = from_z.at[group(g), (core + other) % CORES, d]
                dst = landed.at[group(g), d, core]
                if d or other:
                    remote(src, dst, y_send, y_recv.at[g], at(dy=d, dcore=other))
                else:
                    pltpu.make_async_copy(src, dst, y_recv.at[g]).start()

    def to_x(g):
        wait_bytes(landed.at[group(g)], y_recv.at[g])
        panels[0, lines(g)] = landed[group(g)].reshape(-1, width)
        remote(panels.at[0, lines(g)], panels.at[1, lines(g)], x_send, x1_recv.at[g], at(dx=1))
        remote(panels.at[0, lines(g)], panels.at[2, lines(g)], x_send, x2_recv.at[g], at(dx=-1))

    def key_columns():
        wait_bytes(key_x.at[pl.ds(1, HELD - 1)], key_recv_sem.at[2])
        shape = (Z, ROWS_Z, 128)
        for p in range(HELD):
            spread = jnp.broadcast_to(key_x[p].reshape(Z, 1, 128), shape)
            column = jnp.sum(
                jnp.where(iota(shape, 2) == iota(shape, 1), spread, 0.0),
                axis=2,
                keepdims=True,
            )
            key_cols[p] = jnp.broadcast_to(column, shape).reshape(PANEL, 128)
        for p in range(HELD - 1):
            key_rows[p] = jnp.transpose(key_cols[p])[0:1, :]

    key_steps = {KEY_STEP: keys_to_y, KEY_STEP + 1: keys_to_x, KEY_STEP + 2: key_columns}
    for step in range(GROUPS + LAG_X):
        if step < GROUPS:
            to_y(step)
        if step >= LAG_X:
            to_x(step - LAG_X)
        if step in key_steps:
            key_steps[step]()

    half = Z // 2

    def arrived(low, high):
        for g, (first, last) in enumerate(SPANS):
            if low <= first < high:
                wait_bytes(panels.at[1, lines(g)], x1_recv.at[g])
                wait_bytes(panels.at[2, lines(g)], x2_recv.at[g])

    def largest(query, best, tiles):
        def tile(step, best):
            p, h = tiles(step)
            at_rows = pl.ds(h * half * ROWS_Z, half * ROWS_Z)
            scores = dot_t(panels[p, at_rows, :], panels[query])
            earlier = key_cols[p, at_rows, :][:, 0:1] < key_rows[query]
            scores = jnp.where(earlier, scores, -1.0)
            return jnp.maximum(best, jnp.max(scores, axis=0, keepdims=True))

        return lambda count: lax.fori_loop(0, count, tile, best)

    none = jnp.full((1, PANEL), -1.0, jnp.float32)
    best = largest(0, none, lambda step: (0, step))(2)
    arrived(0, half)
    best = largest(0, best, lambda step: (1 + step, 0))(2)
    arrived(half, Z)
    far = largest(1, none, lambda step: (2, step))(2)
    for i in range(PANEL // 128):
        far_send[i] = far[:, i * 128 : (i + 1) * 128]
    remote(far_send, far_recv, far_sem.at[0], far_sem.at[1], at(dx=-1))
    best = largest(0, best, lambda step: (1 + step, 1))(2)
    wait_bytes(far_recv, far_sem.at[1])

    for i in range(PANEL // 128):
        result[i] = jnp.maximum(best[:, i * 128 : (i + 1) * 128], far_recv[i])
    for a in range(Z - 1, 0, -1):
        remote(
            result.at[a // 4],
            ret_z.at[a],
            ret_send_sem.at[0],
            ret_recv_sem.at[0],
            at(dz=-z_offset(a)),
        )
    spot = a_of * ROWS_Z + dy * BLOCK + core * SLOTS + slot
    chosen = (iota((128, rows), 0) == spot % 128).astype(jnp.float32)
    wanted = iota((CORES * Z, rows), 0) == owner_core * Z + a_of
    ret_z[0] = result[0]
    wait_bytes(ret_z.at[pl.ds(1, Z - 1)], ret_recv_sem.at[0])
    for d in range(Y):
        for other in range(CORES):
            if d or other:
                remote(
                    ret_z,
                    ret_y.at[core * Y + d],
                    ret_send_sem.at[1],
                    ret_recv_sem.at[1],
                    at(dy=-d, dcore=other),
                )
    ret_y[core * Y] = ret_z[...]
    wait_bytes(ret_y.at[pl.ds(1, CORES * Y - 1)], ret_recv_sem.at[1])
    table = []
    for c in range(CORES):
        merged = jnp.zeros((Z, 128), jnp.float32)
        for d in range(Y):
            merged += jnp.where(lane % ROWS_Z // BLOCK == d, ret_y[c * Y + d].reshape(Z, 128), 0.0)
        table.append(merged)
    table = jnp.concatenate(table, axis=0)
    found = jnp.dot(
        table, chosen, precision=lax.Precision.HIGHEST, preferred_element_type=jnp.float32
    )
    found = jnp.where(wanted, found, 0.0)
    out_ref[...] = jnp.sum(found, axis=0, keepdims=True)

    wait_bytes(from_z.at[pl.ds(1, Z - 1)], z_send)
    wait_bytes(landed.at[pl.ds(0, Z - Z // (Y * CORES))], y_send)
    wait_bytes(panels.at[pl.ds(1, HELD - 1)], x_send)
    wait_bytes(far_send, far_sem.at[0])
    wait_bytes(key_z.at[pl.ds(1, Z - 1)], key_send_sem.at[0])
    wait_bytes(key_y.at[pl.ds(1, CORES * Y - 1)], key_send_sem.at[1])
    wait_bytes(key_x.at[pl.ds(1, HELD - 1)], key_send_sem.at[2])
    wait_bytes(ret_z.at[pl.ds(1, Z - 1)], ret_send_sem.at[0])
    wait_bytes(ret_y.at[pl.ds(1, CORES * Y - 1)], ret_send_sem.at[1])


def body(embeddings, cluster, order_rank):
    rows, width = embeddings.shape
    vmem = pl.BlockSpec(memory_space=pltpu.VMEM)
    dma = pltpu.SemaphoreType.DMA
    found = pl.pallas_call(
        kernel,
        out_shape=jax.ShapeDtypeStruct((1, rows), jnp.float32),
        in_specs=[pl.BlockSpec(memory_space=pl.ANY)] * 3,
        out_specs=vmem,
        scratch_shapes=[
            pltpu.VMEM((rows, width), jnp.bfloat16),
            pltpu.VMEM((rows,), jnp.int32),
            pltpu.VMEM((rows,), jnp.int32),
            pltpu.VMEM((rows, width), jnp.bfloat16),
            pltpu.VMEM((Z, CORES, Y, SLOTS, width), jnp.bfloat16),
            pltpu.VMEM((Z, CORES, Y, SLOTS, width), jnp.bfloat16),
            pltpu.VMEM((Z, Y, CORES, SLOTS, width), jnp.bfloat16),
            pltpu.VMEM((HELD, PANEL, width), jnp.bfloat16),
            pltpu.VMEM((Z, 1, 128), jnp.float32),
            pltpu.VMEM((Z, 1, 128), jnp.float32),
            pltpu.VMEM((CORES * Y, Z, 1, 128), jnp.float32),
            pltpu.VMEM((HELD, Z, 128), jnp.float32),
            pltpu.VMEM((HELD, PANEL, 128), jnp.float32),
            pltpu.VMEM((HELD - 1, 1, PANEL), jnp.float32),
            pltpu.VMEM((PANEL // 128, 1, 128), jnp.float32),
            pltpu.VMEM((Z, 1, 128), jnp.float32),
            pltpu.VMEM((CORES * Y, Z, 1, 128), jnp.float32),
            dma,
            dma((GROUPS,)),
            dma,
            dma((GROUPS,)),
            dma,
            dma((GROUPS,)),
            dma((GROUPS,)),
            dma((3,)),
            dma((3,)),
            dma((2,)),
            dma((2,)),
            dma((3,)),
            pltpu.VMEM((PANEL // 128, 1, 128), jnp.float32),
            pltpu.VMEM((PANEL // 128, 1, 128), jnp.float32),
            dma((2,)),
            pltpu.SemaphoreType.REGULAR,
        ],
        compiler_params=pltpu.CompilerParams(
            collective_id=0, has_side_effects=True, vmem_limit_bytes=60 * 1024 * 1024
        ),
    )(embeddings, cluster, order_rank)
    return found.reshape(rows)


def solution(mesh):
    return jax.shard_map(
        body,
        mesh=mesh,
        in_specs=(P(("dp", "helper"), None), P(("dp", "helper")), P(("dp", "helper"))),
        out_specs=P(("dp", "helper")),
        check_vma=False,
    )
```

```python
import functools

import jax
import jax.numpy as jnp
from jax import lax
from jax.experimental import pallas as pl
from jax.experimental.pallas import tpu as pltpu
from jax.sharding import PartitionSpec as P

MESH = pl.DeviceIdType.MESH
Y, Z, CORES, X = 4, 16, 2, 4
SLOTS = 4
BLOCK = CORES * SLOTS
ROWS_Z = Y * BLOCK
PANEL = Z * ROWS_Z
SPANS = tuple((low, low + 2) for low in range(0, Z, 2))
GROUPS = len(SPANS)
NEAR = 8
FAR_FIRST = (2, 1, 3, 0)
KEY_STEP = 2
LAG_X = 1
HELD = 3
EMPTY = 8388608.0


def z_offset(index):
    return (index + 1) // 2 if index % 2 else -(index // 2)


def wait_bytes(ref, sem):
    pltpu.make_async_copy(ref, ref, sem).wait()


def iota(shape, dim):
    return lax.broadcasted_iota(jnp.int32, shape, dim)


def dot_t(lhs, rhs):
    return lax.dot_general(lhs, rhs, (((1,), (1,)), ((), ())), preferred_element_type=jnp.float32)


def kernel(
    emb_hbm,
    cluster_hbm,
    rank_hbm,
    out_ref,
    emb_ref,
    cluster_ref,
    rank_ref,
    units,
    send_z,
    from_z,
    landed,
    panels,
    key_send,
    key_z,
    key_y,
    key_x,
    key_cols,
    key_rows,
    result,
    ret_z,
    ret_y,
    z_send,
    z_recv,
    y_send,
    y_recv,
    x_send,
    x1_recv,
    x2_recv,
    key_send_sem,
    key_recv_sem,
    ret_send_sem,
    ret_recv_sem,
    load_sem,
    far_send,
    far_recv,
    far_sem,
    all_in,
):
    dp, hx = lax.axis_index("dp"), lax.axis_index("helper")
    core, chip = dp % CORES, dp // CORES
    y, z = chip // Z, chip % Z

    def at(dy=0, dz=0, dx=0, dcore=0):
        chip_to = ((y + dy + Y) % Y) * Z + (z + dz + Z) % Z
        return (chip_to * CORES + (core + dcore) % CORES, (hx + dx + X) % X)

    def remote(src, dst, send_sem, recv_sem, to):
        pltpu.make_async_remote_copy(
            src_ref=src,
            dst_ref=dst,
            send_sem=send_sem,
            recv_sem=recv_sem,
            device_id=to,
            device_id_type=MESH,
        ).start()

    loads = [
        pltpu.make_async_copy(src, dst, load_sem.at[i])
        for i, (src, dst) in enumerate(
            ((cluster_hbm, cluster_ref), (rank_hbm, rank_ref), (emb_hbm, emb_ref))
        )
    ]
    for load in loads:
        load.start()
    barrier = pltpu.get_barrier_semaphore()
    peers = [at(dz=z_offset(a)) for a in range(NEAR, 0, -1)]
    peers += [at(dy=d) for d in range(1, Y)] + [at(dy=d, dcore=1) for d in range(Y)]
    peers += [at(dx=1), at(dx=-1)]
    for peer in peers:
        pl.semaphore_signal(barrier, inc=1, device_id=peer, device_id_type=MESH)

    rows, width = emb_ref.shape
    loads[0].wait()
    loads[1].wait()
    cluster = cluster_ref[...].reshape(1, rows)
    rank = rank_ref[...].reshape(1, rows)
    across = jnp.broadcast_to(cluster, (rows, rows))
    down = jnp.transpose(across)
    same_before = (down == across) & (iota((rows, rows), 0) < iota((rows, rows), 1))
    slot = jnp.sum(same_before.astype(jnp.float32), axis=0, keepdims=True).astype(jnp.int32)
    owner_core, owner_chip = cluster % CORES, cluster // CORES
    dy = (owner_chip // Z - y + Y) % Y
    dz = (owner_chip % Z - z + Z) % Z
    a_of = jnp.where(dz == 0, 0, jnp.where(dz <= Z // 2, 2 * dz - 1, 2 * (Z - dz)))
    place = (owner_core * Y + dy) * SLOTS + slot
    target = a_of * ROWS_Z + place

    loads[2].wait()
    values = emb_ref[...].astype(jnp.float32)
    scale = lax.rsqrt(jnp.sum(values * values, axis=-1, keepdims=True) + 1e-06)
    units[...] = (values * scale).astype(jnp.bfloat16)
    chunk = 4 * ROWS_Z
    for first in range(0, Z, 4):
        pick = (iota((chunk, rows), 0) + first * ROWS_Z == target).astype(jnp.float32)
        picked = jnp.dot(
            pick.astype(jnp.bfloat16), units[...], preferred_element_type=jnp.float32
        )
        picked = picked.astype(jnp.bfloat16).reshape(4, CORES, Y, SLOTS, width)
        for i in range(4):
            if first + i:
                send_z[first + i] = picked[i]
            else:
                from_z[0] = picked[0]

    def group_of(a):
        return next(g for g, (low, high) in enumerate(SPANS) if low <= a < high)

    def release(first, last):
        for a in range(first, last):
            send_key(a)
        for a in range(first, last):
            send_rows(a)

    def send_key(a):
        remote(
            key_send.at[a],
            key_z.at[a],
            key_send_sem.at[0],
            key_recv_sem.at[0],
            at(dz=z_offset(a)),
        )

    def send_rows(a):
        remote(
            send_z.at[a], from_z.at[a], z_send, z_recv.at[group_of(a)], at(dz=z_offset(a))
        )

    key = rank * (Z * Y * CORES * X * SLOTS) + (dp * X + hx) * SLOTS + slot + 1
    parts = [key // 16384, key // 128 % 128, key % 128]
    lane = iota((128, rows), 0)
    spread = jnp.where(
        lane < ROWS_Z, parts[0], jnp.where(lane < 2 * ROWS_Z, parts[1], parts[2])
    )
    spread = jnp.where((lane % ROWS_Z == place) & (lane < 3 * ROWS_Z), spread, 0)
    pick = (iota((Z, rows), 0) == a_of).astype(jnp.float32).astype(jnp.bfloat16)
    keys = dot_t(pick, spread.astype(jnp.float32).astype(jnp.bfloat16))
    key_send[...] = keys.reshape(Z, 1, 128)
    key_z[0] = keys[0:1]
    pl.semaphore_wait(barrier, len(peers))
    for dz in (Z // 4, -(Z // 4)):
        pl.semaphore_signal(all_in, inc=1, device_id=at(dz=dz), device_id_type=MESH)
    release(1, NEAR + 1)
    pl.semaphore_wait(all_in, 2)
    release(NEAR + 1, Z)

    lane = iota((Z, 128), 1)

    def keys_to_y():
        wait_bytes(key_z.at[pl.ds(1, Z - 1)], key_recv_sem.at[0])
        for d in range(Y):
            for other in range(CORES):
                if d or other:
                    remote(
                        key_z,
                        key_y.at[core * Y + d],
                        key_send_sem.at[1],
                        key_recv_sem.at[1],
                        at(dy=d, dcore=other),
                    )
        key_y[core * Y] = key_z[...]

    def keys_to_x():
        wait_bytes(key_y.at[pl.ds(1, CORES * Y - 1)], key_recv_sem.at[1])
        merged = jnp.zeros((Z, 128), jnp.float32)
        for c in range(CORES):
            for d in range(Y):
                shift = (128 + SLOTS * (d + c) - Y * SLOTS * core) % 128
                moved = pltpu.roll(key_y[c * Y + d].reshape(Z, 128), shift, 1)
                merged += jnp.where(lane % ROWS_Z // SLOTS == CORES * d + c, moved, 0.0)
        merged = (
            merged * 16384.0
            + pltpu.roll(merged, 128 - ROWS_Z, 1) * 128.0
            + pltpu.roll(merged, 128 - 2 * ROWS_Z, 1)
        )
        key_x[0] = jnp.where(merged == 0.0, EMPTY, merged)
        for place, dx in ((1, 1), (2, -1)):
            remote(
                key_x.at[0], key_x.at[place], key_send_sem.at[2], key_recv_sem.at[2], at(dx=dx)
            )

    def group(g):
        return pl.ds(SPANS[g][0], SPANS[g][1] - SPANS[g][0])

    def lines(g):
        return pl.ds(SPANS[g][0] * ROWS_Z, (SPANS[g][1] - SPANS[g][0]) * ROWS_Z)

    def to_y(g):
        low, high = SPANS[g]
        low = max(low, 1)
        wait_bytes(from_z.at[pl.ds(low, high - low)], z_recv.at[g])
        for d in FAR_FIRST:
            for other in (1, 0):
                src = from_z.at[group(g), (core + other) % CORES, d]
                dst = landed.at[group(g), d, core]
                if d or other:
                    remote(src, dst, y_send, y_recv.at[g], at(dy=d, dcore=other))
                else:
                    pltpu.make_async_copy(src, dst, y_recv.at[g]).start()

    def to_x(g):
        wait_bytes(landed.at[group(g)], y_recv.at[g])
        panels[0, lines(g)] = landed[group(g)].reshape(-1, width)
        remote(panels.at[0, lines(g)], panels.at[1, lines(g)], x_send, x1_recv.at[g], at(dx=1))
        remote(panels.at[0, lines(g)], panels.at[2, lines(g)], x_send, x2_recv.at[g], at(dx=-1))

    def key_columns():
        wait_bytes(key_x.at[pl.ds(1, HELD - 1)], key_recv_sem.at[2])
        shape = (Z, ROWS_Z, 128)
        for p in range(HELD):
            spread = jnp.broadcast_to(key_x[p].reshape(Z, 1, 128), shape)
            column = jnp.sum(
                jnp.where(iota(shape, 2) == iota(shape, 1), spread, 0.0),
                axis=2,
                keepdims=True,
            )
            key_cols[p] = jnp.broadcast_to(column, shape).reshape(PANEL, 128)
        for p in range(HELD - 1):
            key_rows[p] = jnp.transpose(key_cols[p])[0:1, :]

    key_steps = {KEY_STEP: keys_to_y, KEY_STEP + 1: keys_to_x, KEY_STEP + 2: key_columns}
    for step in range(GROUPS + LAG_X):
        if step < GROUPS:
            to_y(step)
        if step >= LAG_X:
            to_x(step - LAG_X)
        if step in key_steps:
            key_steps[step]()

    half = Z // 2

    def arrived(low, high):
        for g, (first, last) in enumerate(SPANS):
            if low <= first < high:
                wait_bytes(panels.at[1, lines(g)], x1_recv.at[g])
                wait_bytes(panels.at[2, lines(g)], x2_recv.at[g])

    def largest(query, best, tiles):
        def tile(step, best):
            p, h = tiles(step)
            at_rows = pl.ds(h * half * ROWS_Z, half * ROWS_Z)
            scores = dot_t(panels[p, at_rows, :], panels[query])
            earlier = key_cols[p, at_rows, :][:, 0:1] < key_rows[query]
            scores = jnp.where(earlier, scores, -1.0)
            return jnp.maximum(best, jnp.max(scores, axis=0, keepdims=True))

        return lambda count: lax.fori_loop(0, count, tile, best)

    none = jnp.full((1, PANEL), -1.0, jnp.float32)
    best = largest(0, none, lambda step: (0, step))(2)
    arrived(0, half)
    best = largest(0, best, lambda step: (1 + step, 0))(2)
    arrived(half, Z)
    far = largest(1, none, lambda step: (2, step))(2)
    for i in range(PANEL // 128):
        far_send[i] = far[:, i * 128 : (i + 1) * 128]
    remote(far_send, far_recv, far_sem.at[0], far_sem.at[1], at(dx=-1))
    best = largest(0, best, lambda step: (1 + step, 1))(2)
    wait_bytes(far_recv, far_sem.at[1])

    for i in range(PANEL // 128):
        result[i] = jnp.maximum(best[:, i * 128 : (i + 1) * 128], far_recv[i])
    for a in range(Z - 1, 0, -1):
        remote(
            result.at[a // 4],
            ret_z.at[a],
            ret_send_sem.at[0],
            ret_recv_sem.at[0],
            at(dz=-z_offset(a)),
        )
    spot = a_of * ROWS_Z + dy * BLOCK + core * SLOTS + slot
    chosen = (iota((128, rows), 0) == spot % 128).astype(jnp.float32)
    wanted = iota((CORES * Z, rows), 0) == owner_core * Z + a_of
    ret_z[0] = result[0]
    wait_bytes(ret_z.at[pl.ds(1, Z - 1)], ret_recv_sem.at[0])
    for d in FAR_FIRST:
        for other in (1, 0):
            if d or other:
                remote(
                    ret_z,
                    ret_y.at[core * Y + d],
                    ret_send_sem.at[1],
                    ret_recv_sem.at[1],
                    at(dy=-d, dcore=other),
                )
    ret_y[core * Y] = ret_z[...]
    wait_bytes(ret_y.at[pl.ds(1, CORES * Y - 1)], ret_recv_sem.at[1])
    table = []
    for c in range(CORES):
        merged = jnp.zeros((Z, 128), jnp.float32)
        for d in range(Y):
            merged += jnp.where(lane % ROWS_Z // BLOCK == d, ret_y[c * Y + d].reshape(Z, 128), 0.0)
        table.append(merged)
    table = jnp.concatenate(table, axis=0)
    found = jnp.dot(
        table, chosen, precision=lax.Precision.HIGHEST, preferred_element_type=jnp.float32
    )
    found = jnp.where(wanted, found, 0.0)
    out_ref[...] = jnp.sum(found, axis=0, keepdims=True)

    wait_bytes(from_z.at[pl.ds(1, Z - 1)], z_send)
    wait_bytes(landed.at[pl.ds(0, Z - Z // (Y * CORES))], y_send)
    wait_bytes(panels.at[pl.ds(1, HELD - 1)], x_send)
    wait_bytes(far_send, far_sem.at[0])
    wait_bytes(key_z.at[pl.ds(1, Z - 1)], key_send_sem.at[0])
    wait_bytes(key_y.at[pl.ds(1, CORES * Y - 1)], key_send_sem.at[1])
    wait_bytes(key_x.at[pl.ds(1, HELD - 1)], key_send_sem.at[2])
    wait_bytes(ret_z.at[pl.ds(1, Z - 1)], ret_send_sem.at[0])
    wait_bytes(ret_y.at[pl.ds(1, CORES * Y - 1)], ret_send_sem.at[1])


def body(embeddings, cluster, order_rank):
    rows, width = embeddings.shape
    vmem = pl.BlockSpec(memory_space=pltpu.VMEM)
    dma = pltpu.SemaphoreType.DMA
    found = pl.pallas_call(
        kernel,
        out_shape=jax.ShapeDtypeStruct((1, rows), jnp.float32),
        in_specs=[pl.BlockSpec(memory_space=pl.ANY)] * 3,
        out_specs=vmem,
        scratch_shapes=[
            pltpu.VMEM((rows, width), jnp.bfloat16),
            pltpu.VMEM((rows,), jnp.int32),
            pltpu.VMEM((rows,), jnp.int32),
            pltpu.VMEM((rows, width), jnp.bfloat16),
            pltpu.VMEM((Z, CORES, Y, SLOTS, width), jnp.bfloat16),
            pltpu.VMEM((Z, CORES, Y, SLOTS, width), jnp.bfloat16),
            pltpu.VMEM((Z, Y, CORES, SLOTS, width), jnp.bfloat16),
            pltpu.VMEM((HELD, PANEL, width), jnp.bfloat16),
            pltpu.VMEM((Z, 1, 128), jnp.float32),
            pltpu.VMEM((Z, 1, 128), jnp.float32),
            pltpu.VMEM((CORES * Y, Z, 1, 128), jnp.float32),
            pltpu.VMEM((HELD, Z, 128), jnp.float32),
            pltpu.VMEM((HELD, PANEL, 128), jnp.float32),
            pltpu.VMEM((HELD - 1, 1, PANEL), jnp.float32),
            pltpu.VMEM((PANEL // 128, 1, 128), jnp.float32),
            pltpu.VMEM((Z, 1, 128), jnp.float32),
            pltpu.VMEM((CORES * Y, Z, 1, 128), jnp.float32),
            dma,
            dma((GROUPS,)),
            dma,
            dma((GROUPS,)),
            dma,
            dma((GROUPS,)),
            dma((GROUPS,)),
            dma((3,)),
            dma((3,)),
            dma((2,)),
            dma((2,)),
            dma((3,)),
            pltpu.VMEM((PANEL // 128, 1, 128), jnp.float32),
            pltpu.VMEM((PANEL // 128, 1, 128), jnp.float32),
            dma((2,)),
            pltpu.SemaphoreType.REGULAR,
        ],
        compiler_params=pltpu.CompilerParams(
            collective_id=0, has_side_effects=True, vmem_limit_bytes=60 * 1024 * 1024
        ),
    )(embeddings, cluster, order_rank)
    return found.reshape(rows)


def solution(mesh):
    return jax.shard_map(
        body,
        mesh=mesh,
        in_specs=(P(("dp", "helper"), None), P(("dp", "helper")), P(("dp", "helper"))),
        out_specs=P(("dp", "helper")),
        check_vma=False,
    )
```

```python
import functools

import jax
import jax.numpy as jnp
from jax import lax
from jax.experimental import pallas as pl
from jax.experimental.pallas import tpu as pltpu
from jax.sharding import PartitionSpec as P

MESH = pl.DeviceIdType.MESH
Y, Z, CORES, X = 4, 16, 2, 4
SLOTS = 4
BLOCK = CORES * SLOTS
ROWS_Z = Y * BLOCK
PANEL = Z * ROWS_Z
SPANS = tuple((low, low + 2) for low in range(0, Z, 2))
GROUPS = len(SPANS)
NEAR = 4
FAR_FIRST = (2, 1, 3, 0)
KEY_STEP = 2
LAG_X = 1
HELD = 3
EMPTY = 8388608.0


def z_offset(index):
    return (index + 1) // 2 if index % 2 else -(index // 2)


def wait_bytes(ref, sem):
    pltpu.make_async_copy(ref, ref, sem).wait()


def iota(shape, dim):
    return lax.broadcasted_iota(jnp.int32, shape, dim)


def dot_t(lhs, rhs):
    return lax.dot_general(lhs, rhs, (((1,), (1,)), ((), ())), preferred_element_type=jnp.float32)


def kernel(
    emb_hbm,
    cluster_hbm,
    rank_hbm,
    out_ref,
    emb_ref,
    cluster_ref,
    rank_ref,
    units,
    send_z,
    from_z,
    landed,
    panels,
    key_send,
    key_z,
    key_y,
    key_x,
    key_cols,
    key_rows,
    result,
    ret_z,
    ret_y,
    z_send,
    z_recv,
    y_send,
    y_recv,
    x_send,
    x1_recv,
    x2_recv,
    key_send_sem,
    key_recv_sem,
    ret_send_sem,
    ret_recv_sem,
    load_sem,
    far_send,
    far_recv,
    far_sem,
    wider,
):
    dp, hx = lax.axis_index("dp"), lax.axis_index("helper")
    core, chip = dp % CORES, dp // CORES
    y, z = chip // Z, chip % Z

    def at(dy=0, dz=0, dx=0, dcore=0):
        chip_to = ((y + dy + Y) % Y) * Z + (z + dz + Z) % Z
        return (chip_to * CORES + (core + dcore) % CORES, (hx + dx + X) % X)

    def remote(src, dst, send_sem, recv_sem, to):
        pltpu.make_async_remote_copy(
            src_ref=src,
            dst_ref=dst,
            send_sem=send_sem,
            recv_sem=recv_sem,
            device_id=to,
            device_id_type=MESH,
        ).start()

    loads = [
        pltpu.make_async_copy(src, dst, load_sem.at[i])
        for i, (src, dst) in enumerate(
            ((cluster_hbm, cluster_ref), (rank_hbm, rank_ref), (emb_hbm, emb_ref))
        )
    ]
    for load in loads:
        load.start()
    barrier = pltpu.get_barrier_semaphore()
    peers = [at(dz=z_offset(a)) for a in range(NEAR, 0, -1)]
    peers += [at(dy=d) for d in range(1, Y)] + [at(dy=d, dcore=1) for d in range(Y)]
    peers += [at(dx=1), at(dx=-1)]
    for peer in peers:
        pl.semaphore_signal(barrier, inc=1, device_id=peer, device_id_type=MESH)

    rows, width = emb_ref.shape
    loads[0].wait()
    loads[1].wait()
    cluster = cluster_ref[...].reshape(1, rows)
    rank = rank_ref[...].reshape(1, rows)
    across = jnp.broadcast_to(cluster, (rows, rows))
    down = jnp.transpose(across)
    same_before = (down == across) & (iota((rows, rows), 0) < iota((rows, rows), 1))
    slot = jnp.sum(same_before.astype(jnp.float32), axis=0, keepdims=True).astype(jnp.int32)
    owner_core, owner_chip = cluster % CORES, cluster // CORES
    dy = (owner_chip // Z - y + Y) % Y
    dz = (owner_chip % Z - z + Z) % Z
    a_of = jnp.where(dz == 0, 0, jnp.where(dz <= Z // 2, 2 * dz - 1, 2 * (Z - dz)))
    place = (owner_core * Y + dy) * SLOTS + slot
    target = a_of * ROWS_Z + place

    loads[2].wait()
    values = emb_ref[...].astype(jnp.float32)
    scale = lax.rsqrt(jnp.sum(values * values, axis=-1, keepdims=True) + 1e-06)
    units[...] = (values * scale).astype(jnp.bfloat16)
    chunk = 4 * ROWS_Z
    for first in range(0, Z, 4):
        pick = (iota((chunk, rows), 0) + first * ROWS_Z == target).astype(jnp.float32)
        picked = jnp.dot(
            pick.astype(jnp.bfloat16), units[...], preferred_element_type=jnp.float32
        )
        picked = picked.astype(jnp.bfloat16).reshape(4, CORES, Y, SLOTS, width)
        for i in range(4):
            if first + i:
                send_z[first + i] = picked[i]
            else:
                from_z[0] = picked[0]

    def group_of(a):
        return next(g for g, (low, high) in enumerate(SPANS) if low <= a < high)

    def release(first, last):
        for a in range(first, last):
            send_key(a)
        for a in range(first, last):
            send_rows(a)

    def send_key(a):
        remote(
            key_send.at[a],
            key_z.at[a],
            key_send_sem.at[0],
            key_recv_sem.at[0],
            at(dz=z_offset(a)),
        )

    def send_rows(a):
        remote(
            send_z.at[a], from_z.at[a], z_send, z_recv.at[group_of(a)], at(dz=z_offset(a))
        )

    key = rank * (Z * Y * CORES * X * SLOTS) + (dp * X + hx) * SLOTS + slot + 1
    parts = [key // 16384, key // 128 % 128, key % 128]
    lane = iota((128, rows), 0)
    spread = jnp.where(
        lane < ROWS_Z, parts[0], jnp.where(lane < 2 * ROWS_Z, parts[1], parts[2])
    )
    spread = jnp.where((lane % ROWS_Z == place) & (lane < 3 * ROWS_Z), spread, 0)
    pick = (iota((Z, rows), 0) == a_of).astype(jnp.float32).astype(jnp.bfloat16)
    keys = dot_t(pick, spread.astype(jnp.float32).astype(jnp.bfloat16))
    key_send[...] = keys.reshape(Z, 1, 128)
    key_z[0] = keys[0:1]
    pl.semaphore_wait(barrier, len(peers))
    first, reach = 1, NEAR // 2
    for step in range(2):
        for dz in (reach, -reach):
            pl.semaphore_signal(
                wider.at[step], inc=1, device_id=at(dz=dz), device_id_type=MESH
            )
        release(first, 2 * reach + 1)
        pl.semaphore_wait(wider.at[step], 2)
        first, reach = 2 * reach + 1, 2 * reach
    release(first, Z)

    lane = iota((Z, 128), 1)

    def keys_to_y():
        wait_bytes(key_z.at[pl.ds(1, Z - 1)], key_recv_sem.at[0])
        for d in range(Y):
            for other in range(CORES):
                if d or other:
                    remote(
                        key_z,
                        key_y.at[core * Y + d],
                        key_send_sem.at[1],
                        key_recv_sem.at[1],
                        at(dy=d, dcore=other),
                    )
        key_y[core * Y] = key_z[...]

    def keys_to_x():
        wait_bytes(key_y.at[pl.ds(1, CORES * Y - 1)], key_recv_sem.at[1])
        merged = jnp.zeros((Z, 128), jnp.float32)
        for c in range(CORES):
            for d in range(Y):
                shift = (128 + SLOTS * (d + c) - Y * SLOTS * core) % 128
                moved = pltpu.roll(key_y[c * Y + d].reshape(Z, 128), shift, 1)
                merged += jnp.where(lane % ROWS_Z // SLOTS == CORES * d + c, moved, 0.0)
        merged = (
            merged * 16384.0
            + pltpu.roll(merged, 128 - ROWS_Z, 1) * 128.0
            + pltpu.roll(merged, 128 - 2 * ROWS_Z, 1)
        )
        key_x[0] = jnp.where(merged == 0.0, EMPTY, merged)
        for place, dx in ((1, 1), (2, -1)):
            remote(
                key_x.at[0], key_x.at[place], key_send_sem.at[2], key_recv_sem.at[2], at(dx=dx)
            )

    def group(g):
        return pl.ds(SPANS[g][0], SPANS[g][1] - SPANS[g][0])

    def lines(g):
        return pl.ds(SPANS[g][0] * ROWS_Z, (SPANS[g][1] - SPANS[g][0]) * ROWS_Z)

    def to_y(g):
        low, high = SPANS[g]
        low = max(low, 1)
        wait_bytes(from_z.at[pl.ds(low, high - low)], z_recv.at[g])
        for d in FAR_FIRST:
            for other in (1, 0):
                src = from_z.at[group(g), (core + other) % CORES, d]
                dst = landed.at[group(g), d, core]
                if d or other:
                    remote(src, dst, y_send, y_recv.at[g], at(dy=d, dcore=other))
                else:
                    pltpu.make_async_copy(src, dst, y_recv.at[g]).start()

    def to_x(g):
        wait_bytes(landed.at[group(g)], y_recv.at[g])
        panels[0, lines(g)] = landed[group(g)].reshape(-1, width)
        remote(panels.at[0, lines(g)], panels.at[1, lines(g)], x_send, x1_recv.at[g], at(dx=1))
        remote(panels.at[0, lines(g)], panels.at[2, lines(g)], x_send, x2_recv.at[g], at(dx=-1))

    def key_columns():
        wait_bytes(key_x.at[pl.ds(1, HELD - 1)], key_recv_sem.at[2])
        shape = (Z, ROWS_Z, 128)
        for p in range(HELD):
            spread = jnp.broadcast_to(key_x[p].reshape(Z, 1, 128), shape)
            column = jnp.sum(
                jnp.where(iota(shape, 2) == iota(shape, 1), spread, 0.0),
                axis=2,
                keepdims=True,
            )
            key_cols[p] = jnp.broadcast_to(column, shape).reshape(PANEL, 128)
        for p in range(HELD - 1):
            key_rows[p] = jnp.transpose(key_cols[p])[0:1, :]

    key_steps = {KEY_STEP: keys_to_y, KEY_STEP + 1: keys_to_x, KEY_STEP + 2: key_columns}
    for step in range(GROUPS + LAG_X):
        if step < GROUPS:
            to_y(step)
        if step >= LAG_X:
            to_x(step - LAG_X)
        if step in key_steps:
            key_steps[step]()

    half = Z // 2

    def arrived(low, high):
        for g, (first, last) in enumerate(SPANS):
            if low <= first < high:
                wait_bytes(panels.at[1, lines(g)], x1_recv.at[g])
                wait_bytes(panels.at[2, lines(g)], x2_recv.at[g])

    def largest(query, best, tiles):
        def tile(step, best):
            p, h = tiles(step)
            at_rows = pl.ds(h * half * ROWS_Z, half * ROWS_Z)
            scores = dot_t(panels[p, at_rows, :], panels[query])
            earlier = key_cols[p, at_rows, :][:, 0:1] < key_rows[query]
            scores = jnp.where(earlier, scores, -1.0)
            return jnp.maximum(best, jnp.max(scores, axis=0, keepdims=True))

        return lambda count: lax.fori_loop(0, count, tile, best)

    none = jnp.full((1, PANEL), -1.0, jnp.float32)
    best = largest(0, none, lambda step: (0, step))(2)
    arrived(0, half)
    best = largest(0, best, lambda step: (1 + step, 0))(2)
    arrived(half, Z)
    far = largest(1, none, lambda step: (2, step))(2)
    for i in range(PANEL // 128):
        far_send[i] = far[:, i * 128 : (i + 1) * 128]
    remote(far_send, far_recv, far_sem.at[0], far_sem.at[1], at(dx=-1))
    best = largest(0, best, lambda step: (1 + step, 1))(2)
    wait_bytes(far_recv, far_sem.at[1])

    for i in range(PANEL // 128):
        result[i] = jnp.maximum(best[:, i * 128 : (i + 1) * 128], far_recv[i])
    for a in range(Z - 1, 0, -1):
        remote(
            result.at[a // 4],
            ret_z.at[a],
            ret_send_sem.at[0],
            ret_recv_sem.at[0],
            at(dz=-z_offset(a)),
        )
    spot = a_of * ROWS_Z + dy * BLOCK + core * SLOTS + slot
    chosen = (iota((128, rows), 0) == spot % 128).astype(jnp.float32)
    wanted = iota((CORES * Z, rows), 0) == owner_core * Z + a_of
    ret_z[0] = result[0]
    wait_bytes(ret_z.at[pl.ds(1, Z - 1)], ret_recv_sem.at[0])
    for d in FAR_FIRST:
        for other in (1, 0):
            if d or other:
                remote(
                    ret_z,
                    ret_y.at[core * Y + d],
                    ret_send_sem.at[1],
                    ret_recv_sem.at[1],
                    at(dy=-d, dcore=other),
                )
    ret_y[core * Y] = ret_z[...]
    wait_bytes(ret_y.at[pl.ds(1, CORES * Y - 1)], ret_recv_sem.at[1])
    table = []
    for c in range(CORES):
        merged = jnp.zeros((Z, 128), jnp.float32)
        for d in range(Y):
            merged += jnp.where(lane % ROWS_Z // BLOCK == d, ret_y[c * Y + d].reshape(Z, 128), 0.0)
        table.append(merged)
    table = jnp.concatenate(table, axis=0)
    found = jnp.dot(
        table, chosen, precision=lax.Precision.HIGHEST, preferred_element_type=jnp.float32
    )
    found = jnp.where(wanted, found, 0.0)
    out_ref[...] = jnp.sum(found, axis=0, keepdims=True)

    wait_bytes(from_z.at[pl.ds(1, Z - 1)], z_send)
    wait_bytes(landed.at[pl.ds(0, Z - Z // (Y * CORES))], y_send)
    wait_bytes(panels.at[pl.ds(1, HELD - 1)], x_send)
    wait_bytes(far_send, far_sem.at[0])
    wait_bytes(key_z.at[pl.ds(1, Z - 1)], key_send_sem.at[0])
    wait_bytes(key_y.at[pl.ds(1, CORES * Y - 1)], key_send_sem.at[1])
    wait_bytes(key_x.at[pl.ds(1, HELD - 1)], key_send_sem.at[2])
    wait_bytes(ret_z.at[pl.ds(1, Z - 1)], ret_send_sem.at[0])
    wait_bytes(ret_y.at[pl.ds(1, CORES * Y - 1)], ret_send_sem.at[1])


def body(embeddings, cluster, order_rank):
    rows, width = embeddings.shape
    vmem = pl.BlockSpec(memory_space=pltpu.VMEM)
    dma = pltpu.SemaphoreType.DMA
    found = pl.pallas_call(
        kernel,
        out_shape=jax.ShapeDtypeStruct((1, rows), jnp.float32),
        in_specs=[pl.BlockSpec(memory_space=pl.ANY)] * 3,
        out_specs=vmem,
        scratch_shapes=[
            pltpu.VMEM((rows, width), jnp.bfloat16),
            pltpu.VMEM((rows,), jnp.int32),
            pltpu.VMEM((rows,), jnp.int32),
            pltpu.VMEM((rows, width), jnp.bfloat16),
            pltpu.VMEM((Z, CORES, Y, SLOTS, width), jnp.bfloat16),
            pltpu.VMEM((Z, CORES, Y, SLOTS, width), jnp.bfloat16),
            pltpu.VMEM((Z, Y, CORES, SLOTS, width), jnp.bfloat16),
            pltpu.VMEM((HELD, PANEL, width), jnp.bfloat16),
            pltpu.VMEM((Z, 1, 128), jnp.float32),
            pltpu.VMEM((Z, 1, 128), jnp.float32),
            pltpu.VMEM((CORES * Y, Z, 1, 128), jnp.float32),
            pltpu.VMEM((HELD, Z, 128), jnp.float32),
            pltpu.VMEM((HELD, PANEL, 128), jnp.float32),
            pltpu.VMEM((HELD - 1, 1, PANEL), jnp.float32),
            pltpu.VMEM((PANEL // 128, 1, 128), jnp.float32),
            pltpu.VMEM((Z, 1, 128), jnp.float32),
            pltpu.VMEM((CORES * Y, Z, 1, 128), jnp.float32),
            dma,
            dma((GROUPS,)),
            dma,
            dma((GROUPS,)),
            dma,
            dma((GROUPS,)),
            dma((GROUPS,)),
            dma((3,)),
            dma((3,)),
            dma((2,)),
            dma((2,)),
            dma((3,)),
            pltpu.VMEM((PANEL // 128, 1, 128), jnp.float32),
            pltpu.VMEM((PANEL // 128, 1, 128), jnp.float32),
            dma((2,)),
            pltpu.SemaphoreType.REGULAR((2,)),
        ],
        compiler_params=pltpu.CompilerParams(
            collective_id=0, has_side_effects=True, vmem_limit_bytes=60 * 1024 * 1024
        ),
    )(embeddings, cluster, order_rank)
    return found.reshape(rows)


def solution(mesh):
    return jax.shard_map(
        body,
        mesh=mesh,
        in_specs=(P(("dp", "helper"), None), P(("dp", "helper")), P(("dp", "helper"))),
        out_specs=P(("dp", "helper")),
        check_vma=False,
    )
```
